32 devices in a mesh: grp: 4 (over y, x), dev: 8 (over z, core).
Axes of the slice: x: 2, y: 2, z: 4, core: 2. Of those that a mesh axis runs over, the one named last changes fastest.
Arguments:
- spectrum: float32 [1152, 8, 128], P(None, 'dev'), may hold values from 0.05 to 2
- sea_mask: int32 [8, 128], P('dev'), may hold values 0 or 1
- wind: float32 [2, 8, 128], P(None, 'dev'), may hold values from -24 to 24
- currents: float32 [4, 2, 4096], P('grp', None, 'dev'), may hold values from -6 to 6
- coupling: int32 [4, 4096], P('grp', 'dev'), may hold values from 0 to 1023, as said below
Outputs:
- updated: float32 [1152, 8, 128], P(None, 'dev')
- cell_drift: float32 [4, 2, 4096], P('grp', None, 'dev')
The draws below stay inside these ranges and needn't reach their ends.
Inputs may be any that keep to these rules, and one draw needn't show every extreme that they name: `coupling`: an ocean cell's entry names the wave point i * 128 + j that it is averaged into and reads its drift from; cell c lies in grid column i with i equal to c // 512 - 1, c // 512 or c // 512 + 1, periodic over 8 columns. `sea_mask`: 1 marks a sea point.
All inputs are finite; a program needn't handle non-finite values. No bound on the sum of `sea_mask` on one device may be relied on, other than what follows from the above.
Results may differ from the reference program's by a relative error of at most 0.00014.
Values sent between devices are 32-bit elements; how exact they have to be, the bound alone decides.
No kernel may reach another device: no remote copies, remote signals or barrier semaphores. Data moves between devices by JAX's collectives and lax.ppermute only.
A program may use at most 64 MiB of HBM per device.

```python
import math
import jax
import jax.numpy as jnp
from jax import lax

NDIR = 32
CELL_DEV = 512
NB = 1152
NX = 8
NY = 128
CELLS = 4096
N_GRP = 4
N_DEV = 8


def draw_coupling(key, part):
    first_key, second_key = jax.random.split(jax.random.fold_in(key, 11))
    owner = (jnp.arange(CELL_DEV * N_DEV, dtype=jnp.int32) // CELL_DEV)[None, :]
    offset = jax.random.randint(first_key, (N_GRP, CELL_DEV * N_DEV), -1, 2, dtype=jnp.int32)
    target_col = (owner + offset + NX) % NX
    target_row = jax.random.randint(second_key, (N_GRP, CELL_DEV * N_DEV), 0, NY, dtype=jnp.int32)
    return (target_col * NY + target_row).astype(jnp.int32)


def plant(drawn, key, least, largest):
    place = [jax.random.randint(jax.random.fold_in(key, axis), (), 0, length) for axis, length in enumerate(drawn.shape)]
    widest = drawn.shape.index(max(drawn.shape))
    next_to = place[:widest] + [(place[widest] + 1) % drawn.shape[widest]] + place[widest + 1:]
    return drawn.at[tuple(place)].set(least).at[tuple(next_to)].set(largest)


def block_levels(stream_key, dims, cuts, least, top_value):
    def one(position, blocks):
        heights = jax.random.uniform(jax.random.fold_in(jax.random.fold_in(stream_key, 6), position), (blocks,), jnp.float32, least / len(cuts), top_value / len(cuts))
        return jnp.repeat(jnp.exp(heights), dims[position] // blocks).reshape((-1,) + (1,) * (len(dims) - position - 1))

    gain = one(*cuts[0])
    for cut in cuts[1:]:
        gain = gain * one(*cut)
    return gain


def scatter_about(rng, extent, scale, most, pieces=(), kind=jnp.bfloat16):
    array = scale * jax.random.normal(rng, extent, jnp.float32)
    if pieces:
        array = array * block_levels(rng, extent, pieces, -0.22, 0.18)
    return jnp.clip(array, -most, most).astype(kind)


def setup_inputs(seed: int = 0) -> dict:
    key_of = jax.random.split(jax.random.key(seed), 6)
    spectrum = jnp.clip(jnp.exp(math.log(2.0) - 3.6888794 * jax.random.uniform(key_of[0], (NB, NX, NY), jnp.float32) ** block_levels(key_of[0], (NB, NX, NY), ((1, 8),), -0.2, 0.2)), 0.05, 2.0)
    sea_mask = plant((jax.random.randint(key_of[1], (NX, NY), 0, 4) < 3).astype(jnp.int32), jax.random.fold_in(key_of[1], 1), 0, 1)
    wind = scatter_about(key_of[2], (2, NX, NY), 8.0, 24.0, ((1, 8),), jnp.float32)
    currents = scatter_about(key_of[3], (N_GRP, 2, CELLS), 1.5, 6.0, ((0, 4), (2, 8)), jnp.float32)
    coupling = draw_coupling(jax.random.fold_in(key_of[5], 71), 0)
    return {"spectrum": spectrum, "sea_mask": sea_mask, "wind": wind, "currents": currents, "coupling": coupling}


FIRST_FREQ = 0.04
GROWTH = 1.1
SPEED_TOP = 0.45
CURRENT_TOP = 0.2
WIND_GAIN = 0.03
WHITECAP = 0.3
STEEP_SCALE = 0.4
STOKES_GAIN = 3.0


def bin_tables(bin_index):
    freq_level = (bin_index // NDIR).astype(jnp.float32)
    heading = (bin_index % NDIR).astype(jnp.float32) * (2.0 * math.pi / NDIR)
    frequency = FIRST_FREQ * GROWTH ** freq_level
    group_speed = SPEED_TOP * FIRST_FREQ / frequency
    return frequency, jnp.cos(heading), jnp.sin(heading), group_speed


def column(values):
    return values[:, None, None]


def sources(energy, sea_frac, wind, mean_current, frequency, cosine_dir, sine_dir):
    energy = energy * sea_frac
    spacing = 0.1 * frequency
    total_energy = jnp.sum(energy * column(spacing), axis=0)
    moment = jnp.sum(energy * column(spacing * frequency), axis=0)
    is_sea = sea_frac > 0.5
    safe_total = jnp.where(is_sea, total_energy, 1.0)
    mean_freq = jnp.where(is_sea, moment / safe_total, 1.0)
    steepness = STEEP_SCALE * total_energy * mean_freq ** 4
    damping = WHITECAP * (column(frequency) / mean_freq) ** 2 * steepness ** 2
    along_wind = column(cosine_dir) * (wind[0] - mean_current[0]) + column(sine_dir) * (wind[1] - mean_current[1])
    growth = WIND_GAIN * jnp.maximum(0.64 * column(frequency) * along_wind - 1.0, 0.0)
    return energy * (1.0 + growth) / (1.0 + damping)


def transport(west_energy, centre, east_energy, west_flow, centre_flow, east_flow, group_speed, cosine_dir, sine_dir, sea_frac):
    speed_x = column(group_speed * cosine_dir)
    speed_y = column(group_speed * sine_dir)
    face_east = 0.5 * ((speed_x + centre_flow[0]) + (speed_x + east_flow[0]))
    face_west = 0.5 * ((speed_x + west_flow[0]) + (speed_x + centre_flow[0]))
    flux_east = jnp.maximum(face_east, 0.0) * centre + jnp.minimum(face_east, 0.0) * east_energy
    flux_west = jnp.maximum(face_west, 0.0) * west_energy + jnp.minimum(face_west, 0.0) * centre
    speed_north = speed_y + centre_flow[1]
    face_north = 0.5 * (speed_north[:, :, :-1] + speed_north[:, :, 1:])
    flux_north = jnp.maximum(face_north, 0.0) * centre[:, :, :-1] + jnp.minimum(face_north, 0.0) * centre[:, :, 1:]
    flux_north = jnp.pad(flux_north, ((0, 0), (0, 0), (1, 1)))
    return sea_frac * (centre - (flux_east - flux_west) - (flux_north[:, :, 1:] - flux_north[:, :, :-1]))


def stokes_table(frequency, cosine_dir, sine_dir):
    weight = STOKES_GAIN * 0.1 * frequency ** 4
    return jnp.stack([weight * cosine_dir, weight * sine_dir])


def reference(spectrum, sea_mask, wind, currents, coupling):
    bin_count, width_x, width_y = spectrum.shape
    groups = currents.shape[0]
    frequency, cosine_dir, sine_dir, group_speed = bin_tables(jnp.arange(bin_count, dtype=jnp.int32))
    sea_frac = sea_mask.astype(jnp.float32)
    ocean_values = jnp.concatenate([currents[1:], jnp.ones_like(currents[1:, :1])], axis=1)
    ocean_values = jnp.transpose(ocean_values, (0, 2, 1)).reshape(-1, 3)
    targets = coupling[1:].reshape(-1)
    cell_sums = jax.ops.segment_sum(ocean_values, targets, num_segments=width_x * width_y).T.reshape(3, width_x, width_y)
    mean_current = cell_sums[:2] / jnp.maximum(cell_sums[2], 1.0)
    transport_flow = CURRENT_TOP * jnp.tanh(mean_current)
    forced = sources(spectrum, sea_frac, wind, mean_current, frequency, cosine_dir, sine_dir)
    updated = transport(jnp.roll(forced, 1, axis=1), forced, jnp.roll(forced, -1, axis=1),
                        jnp.roll(transport_flow, 1, axis=1), transport_flow, jnp.roll(transport_flow, -1, axis=1),
                        group_speed, cosine_dir, sine_dir, sea_frac)
    stokes_drift = jnp.dot(stokes_table(frequency, cosine_dir, sine_dir), updated.reshape(bin_count, -1),
                           precision=lax.Precision.HIGHEST)
    picked = jnp.transpose(stokes_drift[:, coupling], (1, 0, 2))
    ocean_group = (jnp.arange(groups) > 0).astype(jnp.float32)[:, None, None]
    return updated, picked * ocean_group
```

```python
import functools
import math

import jax
import jax.numpy as jnp
import numpy as np
from jax import lax
from jax.experimental import pallas as pl
from jax.experimental.pallas import tpu as pltpu
from jax.sharding import PartitionSpec as P

NDIR = 32
FIRST_FREQ = 0.04
GROWTH = 1.1
SPEED_TOP = 0.45
CURRENT_TOP = 0.2
WIND_GAIN = 0.03
WHITECAP = 0.3
STEEP_SCALE = 0.4
STOKES_GAIN = 3.0

SLOTS = 4
FIELDS = 8
SUM_X, SUM_Y, COUNT, SEA, WIND_X, WIND_Y, DAMP = range(7)
VMEM = pl.BlockSpec(memory_space=pltpu.VMEM)
SMEM = pl.BlockSpec(memory_space=pltpu.SMEM)


def level_groups(levels):
    for size in (4, 3, 2):
        if levels % size == 0:
            return levels // size, size
    return levels, 1


def slots_of(coupling, width, shape_ref, columns):
    col = lax.div(coupling, jnp.int32(width))
    row = coupling - col * width
    slot = col - shape_ref[0]
    slot = jnp.where(slot < 0, slot + columns, slot)
    slot = jnp.where(slot >= columns, slot - columns, slot)
    return row, slot


def band_kernel(columns, where_ref, coupling_ref, currents_ref, spectrum_ref, sea_ref, wind_ref, band_ref):
    width = spectrum_ref.shape[1]
    bins = spectrum_ref.shape[0]
    is_ocean = where_ref[2] > 0

    @pl.when(is_ocean)
    def _():
        row, slot = slots_of(coupling_ref[...], width, where_ref, columns)
        cells = row.shape[1]
        parts_x, parts_y = [], []
        for comp, parts in ((0, parts_x), (1, parts_y)):
            rest = currents_ref[comp : comp + 1, :]
            for _ in range(3):
                part = rest.astype(jnp.bfloat16).astype(jnp.float32)
                parts.append(part)
                rest = rest - part
        slot_id = lax.broadcasted_iota(jnp.int32, (SLOTS, cells), 0)
        here = jnp.where(slot_id == slot, 1.0, 0.0)
        rows = []
        for part in range(3):
            rows += [here * parts_x[part], here * parts_y[part]]
        rows += [here, jnp.zeros_like(here)]
        values = jnp.concatenate(rows, axis=0).astype(jnp.bfloat16)
        row_id = lax.broadcasted_iota(jnp.int32, (width, cells), 0)
        hot = jnp.where(row_id == row, 1.0, 0.0).astype(jnp.bfloat16)
        sums = lax.dot_general(
            values, hot, (((1,), (1,)), ((), ())), preferred_element_type=jnp.float32
        )
        step = 2 * SLOTS
        band_ref[0:step, :] = sums[0:step] + sums[step : 2 * step] + sums[2 * step : 3 * step]
        band_ref[step : 2 * step, :] = sums[3 * step : 4 * step]
        band_ref[2 * step : 4 * step, :] = jnp.zeros((2 * step, width), jnp.float32)

    @pl.when(jnp.logical_not(is_ocean))
    def _():
        band_ref[...] = jnp.zeros_like(band_ref)
        total = jnp.zeros((8, width), jnp.float32)
        moment = jnp.zeros((8, width), jnp.float32)
        for level in range(bins // NDIR):
            frequency = FIRST_FREQ * GROWTH**level
            block = spectrum_ref[level * NDIR : (level + 1) * NDIR, :]
            block = block[0:8] + block[8:16] + (block[16:24] + block[24:32])
            total += (0.1 * frequency) * block
            moment += (0.1 * frequency * frequency) * block
        sea = sea_ref[...].astype(jnp.float32)
        total = jnp.sum(total, axis=0, keepdims=True) * sea
        moment = jnp.sum(moment, axis=0, keepdims=True) * sea
        is_sea = sea > 0.5
        mean_freq = jnp.where(is_sea, moment / jnp.where(is_sea, total, 1.0), 1.0)
        square = mean_freq * mean_freq
        steep = STEEP_SCALE * total * (square * square)
        damp = WHITECAP * (steep * steep) / square
        own = where_ref[1] + 1
        band_ref[pl.ds(SEA * SLOTS + own, 1), :] = sea
        band_ref[pl.ds(WIND_X * SLOTS + own, 1), :] = wind_ref[0:1, :]
        band_ref[pl.ds(WIND_Y * SLOTS + own, 1), :] = wind_ref[1:2, :]
        band_ref[pl.ds(DAMP * SLOTS + own, 1), :] = damp


def step_kernel(
    where_ref, table_ref, own_ref, mate_ref, other_ref, band_ref, before_ref, after_ref, updated_ref, drift_ref
):
    bins, width = own_ref.shape
    lanes = 8
    odd = where_ref[1]
    slot_own, slot_mate, slot_other = 1 + odd, 2 - odd, 3 * odd

    def field(index, slot):
        base = index * SLOTS
        value = band_ref[pl.ds(base + slot, 1), :]
        low = before_ref[pl.ds(base + jnp.minimum(slot, 1) + 2, 1), :]
        high = after_ref[pl.ds(base + jnp.maximum(slot, 2) - 2, 1), :]
        return value + jnp.where(slot < 2, low, high)

    cosine = [table_ref[8 * k : 8 * k + 8, :] for k in range(4)]
    sine = [table_ref[NDIR + 8 * k : NDIR + 8 * k + 8, :] for k in range(4)]

    def column_state(slot):
        count = jnp.maximum(field(COUNT, slot), 1.0)
        mean_x = field(SUM_X, slot) / count
        mean_y = field(SUM_Y, slot) / count
        rel_x = field(WIND_X, slot) - mean_x
        rel_y = field(WIND_Y, slot) - mean_y
        gain = WIND_GAIN * 0.64
        along = [(gain * rel_x) * cosine[k] + (gain * rel_y) * sine[k] for k in range(4)]
        sea = jnp.broadcast_to(field(SEA, slot), (lanes, width))
        damp = jnp.broadcast_to(field(DAMP, slot), (lanes, width))
        return mean_x, mean_y, along, sea, damp

    own_x, own_y, along_own, sea_own, damp_own = column_state(slot_own)
    mate_x, _, along_mate, sea_mate, damp_mate = column_state(slot_mate)
    other_x, _, along_other, sea_other, damp_other = column_state(slot_other)
    flow_x = CURRENT_TOP * jnp.tanh(own_x)
    flow_y = CURRENT_TOP * jnp.tanh(own_y)
    sign = jnp.where(odd > 0, 1.0, -1.0)
    face_mate = jnp.broadcast_to(
        (0.5 * sign) * (flow_x + CURRENT_TOP * jnp.tanh(mate_x)), (lanes, width)
    )
    face_other = jnp.broadcast_to(
        (-0.5 * sign) * (flow_x + CURRENT_TOP * jnp.tanh(other_x)), (lanes, width)
    )
    flow_y = jnp.broadcast_to(flow_y, (lanes, width))
    face_north = 0.5 * (flow_y + pltpu.roll(flow_y, width - 1, 1))
    inner = jnp.where(
        lax.broadcasted_iota(jnp.int32, (lanes, width), 1) < width - 1, 1.0, 0.0
    )
    signed_cosine = [sign * cosine[k] for k in range(4)]
    outer_count, inner_count = level_groups(bins // NDIR)

    def level_step(index, carry):
        frequency, speed, sums = carry
        sums = list(sums)
        for sub in range(inner_count):
            square = frequency * frequency
            scale_own = sea_own / (1.0 + square * damp_own)
            scale_mate = sea_mate / (1.0 + square * damp_mate)
            scale_other = sea_other / (1.0 + square * damp_other)
            weight = (STOKES_GAIN * 0.1) * (square * square)
            base = (index * inner_count + sub) * NDIR
            for k in range(4):
                rows = pl.ds(pl.multiple_of(base + 8 * k, 8), 8)

                def forced_of(ref, scale, along):
                    grown = jnp.maximum(frequency * along[k] + (1.0 - WIND_GAIN), 1.0)
                    return (ref[rows, :] * scale) * grown

                forced = forced_of(own_ref, scale_own, along_own)
                forced_mate = forced_of(mate_ref, scale_mate, along_mate)
                forced_other = forced_of(other_ref, scale_other, along_other)
                speed_x = speed * signed_cosine[k]
                q_mate = face_mate + speed_x
                q_other = face_other - speed_x
                in_mate = jnp.maximum(q_mate, 0.0)
                in_other = jnp.maximum(q_other, 0.0)
                out = (in_mate - q_mate) + (in_other - q_other)
                north = speed * sine[k] + face_north
                flux = (
                    jnp.maximum(north, 0.0) * forced
                    + jnp.minimum(north, 0.0) * pltpu.roll(forced, width - 1, 1)
                ) * inner
                new = forced - out * forced + (in_mate * forced_mate + in_other * forced_other)
                new = (new - (flux - pltpu.roll(flux, 1, 1))) * sea_own
                updated_ref[rows, :] = new
                sums[k] = sums[k] + weight * new
            frequency = frequency * GROWTH
            speed = speed * (1.0 / GROWTH)
        return frequency, speed, tuple(sums)

    zero = jnp.zeros((lanes, width), jnp.float32)
    start = (jnp.float32(FIRST_FREQ), jnp.float32(SPEED_TOP), (zero,) * 4)
    _, _, sums = lax.fori_loop(0, outer_count, level_step, start)
    drift_x = sums[0] * cosine[0]
    drift_y = sums[0] * sine[0]
    for k in range(1, 4):
        drift_x = drift_x + sums[k] * cosine[k]
        drift_y = drift_y + sums[k] * sine[k]
    drift_ref[0:1, :] = jnp.sum(drift_x, axis=0, keepdims=True)
    drift_ref[1:2, :] = jnp.sum(drift_y, axis=0, keepdims=True)
    drift_ref[2:8, :] = jnp.zeros((6, width), jnp.float32)


def pick_kernel(columns, where_ref, coupling_ref, own_ref, mate_ref, other_ref, cells_ref):
    width = own_ref.shape[1]
    odd = where_ref[1]
    ocean = jnp.where(where_ref[2] > 0, 1.0, 0.0)
    for start in range(0, coupling_ref.shape[1], width):
        part = pl.ds(start, width)
        row, slot = slots_of(coupling_ref[:, part], width, where_ref, columns)
        row = jnp.broadcast_to(row, (8, width))
        own = jnp.take_along_axis(own_ref[...], row, axis=1)[0:2]
        mate = jnp.take_along_axis(mate_ref[...], row, axis=1)[0:2]
        other = jnp.take_along_axis(other_ref[...], row, axis=1)[0:2]
        value = jnp.where(slot == 1 + odd, own, jnp.where(slot == 2 - odd, mate, other))
        cells_ref[:, part] = value * ocean


def direction_table(width):
    heading = np.arange(NDIR) * (2.0 * math.pi / NDIR)
    table = np.concatenate([np.cos(heading), np.sin(heading)]).astype(np.float32)
    return jnp.asarray(np.repeat(table[:, None], width, axis=1))


def body(spectrum, sea_mask, wind, currents, coupling):
    bins, _, width = spectrum.shape
    devices = lax.axis_size("dev")
    groups = lax.axis_size("grp")
    me = lax.axis_index("dev")
    odd = me % 2
    first = me - odd - 1
    where = jnp.stack([first, odd, lax.axis_index("grp")]).astype(jnp.int32)
    mates = [(i, i ^ 1) for i in range(devices)]
    others = [(i, (i + (1 if i % 2 else -1)) % devices) for i in range(devices)]

    def shifted(value, steps):
        return lax.ppermute(value, "dev", [(i, (i + steps) % devices) for i in range(devices)])

    own = spectrum.reshape(bins, width)
    other = lax.ppermute(own, "dev", others)
    mate = lax.ppermute(own, "dev", mates)

    band = pl.pallas_call(
        functools.partial(band_kernel, devices),
        out_shape=jax.ShapeDtypeStruct((FIELDS * SLOTS, width), jnp.float32),
        in_specs=[SMEM] + [VMEM] * 5,
        out_specs=VMEM,
    )(where, coupling, currents[0], own, sea_mask, wind[:, 0])
    band = band + lax.ppermute(band, "dev", mates)
    reach = 1
    while reach < groups:
        band = band + lax.ppermute(band, "grp", [(i, i ^ reach) for i in range(groups)])
        reach *= 2
    before = shifted(band, 2)
    after = shifted(band, -2)

    updated, drift = pl.pallas_call(
        step_kernel,
        out_shape=(
            jax.ShapeDtypeStruct((bins, width), jnp.float32),
            jax.ShapeDtypeStruct((8, width), jnp.float32),
        ),
        in_specs=[SMEM] + [VMEM] * 7,
        out_specs=(VMEM, VMEM),
    )(where, direction_table(width), own, mate, other, band, before, after)

    drift_other = lax.ppermute(drift, "dev", others)
    drift_mate = lax.ppermute(drift, "dev", mates)
    cells = pl.pallas_call(
        functools.partial(pick_kernel, devices),
        out_shape=jax.ShapeDtypeStruct(currents.shape[1:], jnp.float32),
        in_specs=[SMEM] + [VMEM] * 4,
        out_specs=VMEM,
    )(where, coupling, drift, drift_mate, drift_other)
    return updated.reshape(spectrum.shape), cells[None]


def solution(mesh):
    return jax.shard_map(
        body,
        mesh=mesh,
        in_specs=(
            P(None, "dev", None),
            P("dev", None),
            P(None, "dev", None),
            P("grp", None, "dev"),
            P("grp", "dev"),
        ),
        out_specs=(P(None, "dev", None), P("grp", None, "dev")),
        check_vma=False,
    )
```

```python
import functools
import math

import jax
import jax.numpy as jnp
import numpy as np
from jax import lax
from jax.experimental import pallas as pl
from jax.experimental.pallas import tpu as pltpu
from jax.sharding import PartitionSpec as P

NDIR = 32
FIRST_FREQ = 0.04
GROWTH = 1.1
SPEED_TOP = 0.45
CURRENT_TOP = 0.2
WIND_GAIN = 0.03
WHITECAP = 0.3
STEEP_SCALE = 0.4
STOKES_GAIN = 3.0

SLOTS = 4
FIELDS = 8
SUM_X, SUM_Y, COUNT, SEA, WIND_X, WIND_Y, DAMP = range(7)
VMEM = pl.BlockSpec(memory_space=pltpu.VMEM)


def near(*arrays):
    return [pltpu.with_memory_space_constraint(array, pltpu.VMEM) for array in arrays]


def place():
    me = lax.axis_index("dev")
    odd = lax.rem(me, 2)
    return me - odd - 1, odd, lax.axis_index("grp")


def level_groups(levels):
    for size in (4, 3, 2):
        if levels % size == 0:
            return levels // size, size
    return levels, 1


def slots_of(coupling, width, first, columns):
    col = lax.div(coupling, jnp.int32(width))
    row = coupling - col * width
    slot = col - first
    slot = jnp.where(slot < 0, slot + columns, slot)
    slot = jnp.where(slot >= columns, slot - columns, slot)
    return row, slot


def band_kernel(columns, coupling_ref, currents_ref, spectrum_ref, sea_ref, wind_ref, band_ref):
    width = spectrum_ref.shape[1]
    bins = spectrum_ref.shape[0]
    first, odd, group = place()
    is_ocean = group > 0

    @pl.when(is_ocean)
    def _():
        row, slot = slots_of(coupling_ref[...], width, first, columns)
        cells = row.shape[1]
        parts_x, parts_y = [], []
        for comp, parts in ((0, parts_x), (1, parts_y)):
            rest = currents_ref[comp : comp + 1, :]
            for _ in range(3):
                part = rest.astype(jnp.bfloat16).astype(jnp.float32)
                parts.append(part)
                rest = rest - part
        slot_id = lax.broadcasted_iota(jnp.int32, (SLOTS, cells), 0)
        here = jnp.where(slot_id == slot, 1.0, 0.0)
        rows = []
        for part in range(3):
            rows += [here * parts_x[part], here * parts_y[part]]
        rows += [here, jnp.zeros_like(here)]
        values = jnp.concatenate(rows, axis=0).astype(jnp.bfloat16)
        row_id = lax.broadcasted_iota(jnp.int32, (width, cells), 0)
        hot = jnp.where(row_id == row, 1.0, 0.0).astype(jnp.bfloat16)
        sums = lax.dot_general(
            values, hot, (((1,), (1,)), ((), ())), preferred_element_type=jnp.float32
        )
        step = 2 * SLOTS
        band_ref[0:step, :] = sums[0:step] + sums[step : 2 * step] + sums[2 * step : 3 * step]
        band_ref[step : 2 * step, :] = sums[3 * step : 4 * step]
        band_ref[2 * step : 4 * step, :] = jnp.zeros((2 * step, width), jnp.float32)

    @pl.when(jnp.logical_not(is_ocean))
    def _():
        band_ref[...] = jnp.zeros_like(band_ref)
        total = jnp.zeros((8, width), jnp.float32)
        moment = jnp.zeros((8, width), jnp.float32)
        for level in range(bins // NDIR):
            frequency = FIRST_FREQ * GROWTH**level
            block = spectrum_ref[level * NDIR : (level + 1) * NDIR, :]
            block = block[0:8] + block[8:16] + (block[16:24] + block[24:32])
            total += (0.1 * frequency) * block
            moment += (0.1 * frequency * frequency) * block
        sea = sea_ref[...].astype(jnp.float32)
        total = jnp.sum(total, axis=0, keepdims=True) * sea
        moment = jnp.sum(moment, axis=0, keepdims=True) * sea
        is_sea = sea > 0.5
        mean_freq = jnp.where(is_sea, moment / jnp.where(is_sea, total, 1.0), 1.0)
        square = mean_freq * mean_freq
        steep = STEEP_SCALE * total * (square * square)
        damp = WHITECAP * (steep * steep) / square
        own = odd + 1
        band_ref[pl.ds(SEA * SLOTS + own, 1), :] = sea
        band_ref[pl.ds(WIND_X * SLOTS + own, 1), :] = wind_ref[0:1, :]
        band_ref[pl.ds(WIND_Y * SLOTS + own, 1), :] = wind_ref[1:2, :]
        band_ref[pl.ds(DAMP * SLOTS + own, 1), :] = damp


def step_kernel(
    table_ref, own_ref, mate_ref, other_ref, band_ref, before_ref, after_ref, updated_ref, drift_ref
):
    bins, width = own_ref.shape
    lanes = 8
    outer_count, inner_count = level_groups(bins // NDIR)
    _, odd, _ = place()
    slot_own, slot_mate, slot_other = 1 + odd, 2 - odd, 3 * odd

    def field(index, slot):
        base = index * SLOTS
        value = band_ref[pl.ds(base + slot, 1), :]
        low = before_ref[pl.ds(base + jnp.minimum(slot, 1) + 2, 1), :]
        high = after_ref[pl.ds(base + jnp.maximum(slot, 2) - 2, 1), :]
        return value + jnp.where(slot < 2, low, high)

    cosine = [table_ref[8 * k : 8 * k + 8, :] for k in range(4)]
    sine = [table_ref[NDIR + 8 * k : NDIR + 8 * k + 8, :] for k in range(4)]

    def column_state(slot):
        count = jnp.maximum(field(COUNT, slot), 1.0)
        mean_x = field(SUM_X, slot) / count
        mean_y = field(SUM_Y, slot) / count
        rel_x = field(WIND_X, slot) - mean_x
        rel_y = field(WIND_Y, slot) - mean_y
        gain = WIND_GAIN * 0.64
        along = [(gain * rel_x) * cosine[k] + (gain * rel_y) * sine[k] for k in range(4)]
        sea = jnp.broadcast_to(field(SEA, slot), (lanes, width))
        damp = jnp.broadcast_to(field(DAMP, slot), (lanes, width))
        return mean_x, mean_y, along, sea, damp

    own_x, own_y, along_own, sea_own, damp_own = column_state(slot_own)
    mate_x, _, along_mate, sea_mate, damp_mate = column_state(slot_mate)
    other_x, _, along_other, sea_other, damp_other = column_state(slot_other)
    flow_x = CURRENT_TOP * jnp.tanh(own_x)
    flow_y = CURRENT_TOP * jnp.tanh(own_y)
    sign = jnp.where(odd > 0, 1.0, -1.0)
    face_mate = jnp.broadcast_to(
        (0.5 * sign) * (flow_x + CURRENT_TOP * jnp.tanh(mate_x)), (lanes, width)
    )
    face_other = jnp.broadcast_to(
        (-0.5 * sign) * (flow_x + CURRENT_TOP * jnp.tanh(other_x)), (lanes, width)
    )
    flow_y = jnp.broadcast_to(flow_y, (lanes, width))
    face_north = 0.5 * (flow_y + pltpu.roll(flow_y, width - 1, 1))
    inner = jnp.where(
        lax.broadcasted_iota(jnp.int32, (lanes, width), 1) < width - 1, 1.0, 0.0
    )
    signed_cosine = [sign * cosine[k] for k in range(4)]

    def level_step(index, carry):
        frequency, speed, sums = carry
        sums = list(sums)
        for sub in range(inner_count):
            square = frequency * frequency
            scale_own = sea_own / (1.0 + square * damp_own)
            scale_mate = sea_mate / (1.0 + square * damp_mate)
            scale_other = sea_other / (1.0 + square * damp_other)
            weight = (STOKES_GAIN * 0.1) * (square * square)
            base = (index * inner_count + sub) * NDIR
            for k in range(4):
                rows = pl.ds(pl.multiple_of(base + 8 * k, 8), 8)

                def forced_of(ref, scale, along):
                    grown = jnp.maximum(frequency * along[k] + (1.0 - WIND_GAIN), 1.0)
                    return (ref[rows, :] * scale) * grown

                forced = forced_of(own_ref, scale_own, along_own)
                forced_mate = forced_of(mate_ref, scale_mate, along_mate)
                forced_other = forced_of(other_ref, scale_other, along_other)
                speed_x = speed * signed_cosine[k]
                q_mate = face_mate + speed_x
                q_other = face_other - speed_x
                in_mate = jnp.maximum(q_mate, 0.0)
                in_other = jnp.maximum(q_other, 0.0)
                out = (in_mate - q_mate) + (in_other - q_other)
                north = speed * sine[k] + face_north
                flux = (
                    jnp.maximum(north, 0.0) * forced
                    + jnp.minimum(north, 0.0) * pltpu.roll(forced, width - 1, 1)
                ) * inner
                new = forced - out * forced + (in_mate * forced_mate + in_other * forced_other)
                new = (new - (flux - pltpu.roll(flux, 1, 1))) * sea_own
                updated_ref[rows, :] = new
                sums[k] = sums[k] + weight * new
            frequency = frequency * GROWTH
            speed = speed * (1.0 / GROWTH)
        return frequency, speed, tuple(sums)

    zero = jnp.zeros((lanes, width), jnp.float32)
    start = (jnp.float32(FIRST_FREQ), jnp.float32(SPEED_TOP), (zero,) * 4)
    _, _, sums = lax.fori_loop(0, outer_count, level_step, start)
    drift_x = sums[0] * cosine[0]
    drift_y = sums[0] * sine[0]
    for k in range(1, 4):
        drift_x = drift_x + sums[k] * cosine[k]
        drift_y = drift_y + sums[k] * sine[k]
    drift_ref[0:1, :] = jnp.sum(drift_x, axis=0, keepdims=True)
    drift_ref[1:2, :] = jnp.sum(drift_y, axis=0, keepdims=True)
    drift_ref[2:8, :] = jnp.zeros((6, width), jnp.float32)


def pick_kernel(columns, coupling_ref, own_ref, mate_ref, other_ref, cells_ref):
    width = own_ref.shape[1]
    first, odd, group = place()
    ocean = jnp.where(group > 0, 1.0, 0.0)
    for start in range(0, coupling_ref.shape[1], width):
        part = pl.ds(start, width)
        row, slot = slots_of(coupling_ref[:, part], width, first, columns)
        row = jnp.broadcast_to(row, (8, width))
        own = jnp.take_along_axis(own_ref[...], row, axis=1)[0:2]
        mate = jnp.take_along_axis(mate_ref[...], row, axis=1)[0:2]
        other = jnp.take_along_axis(other_ref[...], row, axis=1)[0:2]
        value = jnp.where(slot == 1 + odd, own, jnp.where(slot == 2 - odd, mate, other))
        cells_ref[:, part] = value * ocean


def direction_table(width):
    heading = np.arange(NDIR) * (2.0 * math.pi / NDIR)
    table = np.concatenate([np.cos(heading), np.sin(heading)]).astype(np.float32)
    return jnp.asarray(np.repeat(table[:, None], width, axis=1))


def body(spectrum, sea_mask, wind, currents, coupling):
    bins, _, width = spectrum.shape
    devices = lax.axis_size("dev")
    groups = lax.axis_size("grp")
    mates = [(i, i ^ 1) for i in range(devices)]
    others = [(i, (i + (1 if i % 2 else -1)) % devices) for i in range(devices)]

    def shifted(value, steps):
        return lax.ppermute(value, "dev", [(i, (i + steps) % devices) for i in range(devices)])

    own = spectrum.reshape(bins, width)
    other = lax.ppermute(own, "dev", others)
    mate = lax.ppermute(own, "dev", mates)

    band = pl.pallas_call(
        functools.partial(band_kernel, devices),
        out_shape=pltpu.VMEM((FIELDS * SLOTS, width), jnp.float32),
        in_specs=[VMEM] * 5,
        out_specs=VMEM,
    )(*near(coupling, currents[0], own, sea_mask, wind[:, 0]))
    band = band + lax.ppermute(band, "dev", mates)
    band, mate = lax.optimization_barrier((band, mate))
    reach = 1
    while reach < groups:
        band = band + lax.ppermute(band, "grp", [(i, i ^ reach) for i in range(groups)])
        reach *= 2
    before = shifted(band, 2)
    after = shifted(band, -2)

    updated, drift = pl.pallas_call(
        step_kernel,
        out_shape=(
            pltpu.VMEM((bins, width), jnp.float32),
            pltpu.VMEM((8, width), jnp.float32),
        ),
        in_specs=[VMEM] * 7,
        out_specs=(VMEM, VMEM),
    )(*near(direction_table(width), own, mate, other, band, before, after))

    drift_other = lax.ppermute(drift, "dev", others)
    drift_mate = lax.ppermute(drift, "dev", mates)
    cells = pl.pallas_call(
        functools.partial(pick_kernel, devices),
        out_shape=jax.ShapeDtypeStruct(currents.shape[1:], jnp.float32),
        in_specs=[VMEM] * 4,
        out_specs=VMEM,
    )(*near(coupling, drift, drift_mate, drift_other))
    return updated.reshape(spectrum.shape), cells[None]


def solution(mesh):
    return jax.shard_map(
        body,
        mesh=mesh,
        in_specs=(
            P(None, "dev", None),
            P("dev", None),
            P(None, "dev", None),
            P("grp", None, "dev"),
            P("grp", "dev"),
        ),
        out_specs=(P(None, "dev", None), P("grp", None, "dev")),
        check_vma=False,
    )
```

```python
import functools
import math

import jax
import jax.numpy as jnp
import numpy as np
from jax import lax
from jax.experimental import pallas as pl
from jax.experimental.pallas import tpu as pltpu
from jax.sharding import PartitionSpec as P

NDIR = 32
FIRST_FREQ = 0.04
GROWTH = 1.1
SPEED_TOP = 0.45
CURRENT_TOP = 0.2
WIND_GAIN = 0.03
WHITECAP = 0.3
STEEP_SCALE = 0.4
STOKES_GAIN = 3.0

SLOTS = 4
FIELDS = 8
SUM_X, SUM_Y, COUNT, SEA, WIND_X, WIND_Y, DAMP = range(7)
VMEM = pl.BlockSpec(memory_space=pltpu.VMEM)


def near(*arrays):
    return [pltpu.with_memory_space_constraint(array, pltpu.VMEM) for array in arrays]


def place():
    me = lax.axis_index("dev")
    odd = lax.rem(me, 2)
    return me - odd - 1, odd, lax.axis_index("grp")


def level_groups(levels):
    for size in (4, 3, 2):
        if levels % size == 0:
            return levels // size, size
    return levels, 1


def slots_of(coupling, width, first, columns):
    col = lax.div(coupling, jnp.int32(width))
    row = coupling - col * width
    slot = col - first
    slot = jnp.where(slot < 0, slot + columns, slot)
    slot = jnp.where(slot >= columns, slot - columns, slot)
    return row, slot


def band_kernel(
    columns, coupling_hbm, currents_hbm, spectrum_hbm, sea_hbm, wind_hbm, band_ref,
    coupling_ref, currents_ref, spectrum_ref, sea_ref, wind_ref, sems,
):
    bins, width = spectrum_ref.shape
    first, odd, group = place()
    is_ocean = group > 0

    @pl.when(is_ocean)
    def _():
        copies = [
            pltpu.make_async_copy(coupling_hbm, coupling_ref, sems.at[0]),
            pltpu.make_async_copy(currents_hbm, currents_ref, sems.at[1]),
        ]
        for copy in copies:
            copy.start()
        for copy in copies:
            copy.wait()
        row, slot = slots_of(coupling_ref[...], width, first, columns)
        cells = row.shape[1]
        parts_x, parts_y = [], []
        for comp, parts in ((0, parts_x), (1, parts_y)):
            rest = currents_ref[comp : comp + 1, :]
            for _ in range(3):
                part = rest.astype(jnp.bfloat16).astype(jnp.float32)
                parts.append(part)
                rest = rest - part
        slot_id = lax.broadcasted_iota(jnp.int32, (SLOTS, cells), 0)
        here = jnp.where(slot_id == slot, 1.0, 0.0)
        rows = []
        for part in range(3):
            rows += [here * parts_x[part], here * parts_y[part]]
        rows += [here, jnp.zeros_like(here)]
        values = jnp.concatenate(rows, axis=0).astype(jnp.bfloat16)
        row_id = lax.broadcasted_iota(jnp.int32, (width, cells), 0)
        hot = jnp.where(row_id == row, 1.0, 0.0).astype(jnp.bfloat16)
        sums = lax.dot_general(
            values, hot, (((1,), (1,)), ((), ())), preferred_element_type=jnp.float32
        )
        step = 2 * SLOTS
        band_ref[0:step, :] = sums[0:step] + sums[step : 2 * step] + sums[2 * step : 3 * step]
        band_ref[step : 2 * step, :] = sums[3 * step : 4 * step]
        band_ref[2 * step : 4 * step, :] = jnp.zeros((2 * step, width), jnp.float32)

    @pl.when(jnp.logical_not(is_ocean))
    def _():
        copies = [
            pltpu.make_async_copy(spectrum_hbm, spectrum_ref, sems.at[2]),
            pltpu.make_async_copy(sea_hbm, sea_ref, sems.at[3]),
            pltpu.make_async_copy(wind_hbm, wind_ref, sems.at[4]),
        ]
        for copy in copies:
            copy.start()
        band_ref[...] = jnp.zeros_like(band_ref)
        for copy in copies:
            copy.wait()
        total = jnp.zeros((8, width), jnp.float32)
        moment = jnp.zeros((8, width), jnp.float32)
        for level in range(bins // NDIR):
            frequency = FIRST_FREQ * GROWTH**level
            block = spectrum_ref[level * NDIR : (level + 1) * NDIR, :]
            block = block[0:8] + block[8:16] + (block[16:24] + block[24:32])
            total += (0.1 * frequency) * block
            moment += (0.1 * frequency * frequency) * block
        sea = sea_ref[...].astype(jnp.float32)
        total = jnp.sum(total, axis=0, keepdims=True) * sea
        moment = jnp.sum(moment, axis=0, keepdims=True) * sea
        is_sea = sea > 0.5
        mean_freq = jnp.where(is_sea, moment / jnp.where(is_sea, total, 1.0), 1.0)
        square = mean_freq * mean_freq
        steep = STEEP_SCALE * total * (square * square)
        damp = WHITECAP * (steep * steep) / square
        own = odd + 1
        band_ref[pl.ds(SEA * SLOTS + own, 1), :] = sea
        band_ref[pl.ds(WIND_X * SLOTS + own, 1), :] = wind_ref[0:1, :]
        band_ref[pl.ds(WIND_Y * SLOTS + own, 1), :] = wind_ref[1:2, :]
        band_ref[pl.ds(DAMP * SLOTS + own, 1), :] = damp


def tables_of(table_ref):
    cosine = [table_ref[8 * k : 8 * k + 8, :] for k in range(4)]
    sine = [table_ref[NDIR + 8 * k : NDIR + 8 * k + 8, :] for k in range(4)]
    return cosine, sine


def row_of(total_ref, index, slot):
    return total_ref[pl.ds(index * SLOTS + slot, 1), :]


def flow_of(total_ref, index, slot):
    count = jnp.maximum(row_of(total_ref, COUNT, slot), 1.0)
    return CURRENT_TOP * jnp.tanh(row_of(total_ref, index, slot) / count)


def source_state(total_ref, slot, cosine, sine):
    count = jnp.maximum(row_of(total_ref, COUNT, slot), 1.0)
    gain = WIND_GAIN * 0.64
    rel_x = gain * (row_of(total_ref, WIND_X, slot) - row_of(total_ref, SUM_X, slot) / count)
    rel_y = gain * (row_of(total_ref, WIND_Y, slot) - row_of(total_ref, SUM_Y, slot) / count)
    along = [rel_x * cosine[k] + rel_y * sine[k] for k in range(4)]
    sea = jnp.broadcast_to(row_of(total_ref, SEA, slot), cosine[0].shape)
    damp = jnp.broadcast_to(row_of(total_ref, DAMP, slot), cosine[0].shape)
    return along, sea, damp


def forced_of(energy, scale, frequency, along):
    return (energy * scale) * jnp.maximum(frequency * along + (1.0 - WIND_GAIN), 1.0)


def over_levels(bins, level_body, sums):
    outer_count, inner_count = level_groups(bins // NDIR)

    def step(index, carry):
        frequency, speed, values = carry
        for sub in range(inner_count):
            base = (index * inner_count + sub) * NDIR
            values = level_body(base, frequency, speed, values)
            frequency = frequency * GROWTH
            speed = speed * (1.0 / GROWTH)
        return frequency, speed, values

    start = (jnp.float32(FIRST_FREQ), jnp.float32(SPEED_TOP), sums)
    return lax.fori_loop(0, outer_count, step, start)[2]


def own_column(total_ref, odd, cosine, sine):
    lanes = cosine[0].shape
    width = lanes[1]
    along, sea, damp = source_state(total_ref, 1 + odd, cosine, sine)
    flow_x = flow_of(total_ref, SUM_X, 1 + odd)
    flow_low = flow_of(total_ref, SUM_X, odd)
    flow_high = flow_of(total_ref, SUM_X, 2 + odd)
    flow_y = jnp.broadcast_to(flow_of(total_ref, SUM_Y, 1 + odd), lanes)
    inner = jnp.where(lax.broadcasted_iota(jnp.int32, lanes, 1) < width - 1, 1.0, 0.0)
    return {
        "along": along,
        "sea": sea,
        "damp": damp,
        "cosine": cosine,
        "face_low": jnp.broadcast_to(-0.5 * (flow_low + flow_x), lanes),
        "face_high": jnp.broadcast_to(0.5 * (flow_x + flow_high), lanes),
        "face_north": (0.5 * inner) * (flow_y + pltpu.roll(flow_y, width - 1, 1)),
        "sine": [inner * sine[k] for k in range(4)],
    }


def kept_and_sent(own, energy, scale, frequency, speed, k):
    width = energy.shape[1]
    forced = forced_of(energy, scale, frequency, own["along"][k])
    speed_x = speed * own["cosine"][k]
    to_high = jnp.maximum(own["face_high"] + speed_x, 0.0) * forced
    to_low = jnp.maximum(own["face_low"] - speed_x, 0.0) * forced
    north = speed * own["sine"][k] + own["face_north"]
    flux = jnp.maximum(north, 0.0) * forced
    flux = flux + jnp.minimum(north, 0.0) * pltpu.roll(forced, width - 1, 1)
    keep = (forced - (to_high + to_low)) - (flux - pltpu.roll(flux, 1, 1))
    return keep, to_low, to_high


def home_kernel(table_ref, own_ref, _, band_ref, before_ref, after_ref, out_ref, total_ref):
    bins, width = own_ref.shape
    _, odd, _ = place()
    rows = band_ref.shape[0]
    low = lax.broadcasted_iota(jnp.int32, (rows, width), 0) % SLOTS < 2
    total_ref[...] = band_ref[...] + jnp.where(
        low, pltpu.roll(before_ref[...], rows - 2, 0), pltpu.roll(after_ref[...], 2, 0)
    )
    cosine, sine = tables_of(table_ref)
    lanes = cosine[0].shape
    own = own_column(total_ref, odd, cosine, sine)

    def level(base, frequency, speed, sums):
        kept, lows, highs = (list(part) for part in sums)
        square = frequency * frequency
        scale = own["sea"] / (1.0 + square * own["damp"])
        weight = (STOKES_GAIN * 0.1) * (square * square)
        for k in range(4):
            at = pl.ds(pl.multiple_of(base + 8 * k, 8), 8)
            keep, to_low, to_high = kept_and_sent(own, own_ref[at, :], scale, frequency, speed, k)
            kept[k] = kept[k] + weight * keep
            lows[k] = lows[k] + weight * to_low
            highs[k] = highs[k] + weight * to_high
        return tuple(kept), tuple(lows), tuple(highs)

    zero = (jnp.zeros(lanes, jnp.float32),) * 4
    parts = over_levels(bins, level, (zero, zero, zero))
    out_ref[...] = jnp.zeros_like(out_ref)
    for index, part in enumerate(parts):
        for comp, turn in enumerate((cosine, sine)):
            value = part[0] * turn[0]
            for k in range(1, 4):
                value = value + part[k] * turn[k]
            at = pl.ds((2 * index + comp) * SLOTS + 1 + odd, 1)
            out_ref[at, :] = jnp.sum(value, axis=0, keepdims=True)


def update_kernel(table_ref, own_ref, mate_ref, other_ref, total_ref, updated_ref):
    bins = own_ref.shape[0]
    _, odd, _ = place()
    slot_mate, slot_other = 2 - odd, 3 * odd
    cosine, sine = tables_of(table_ref)
    lanes = cosine[0].shape
    along_mate, sea_mate, damp_mate = source_state(total_ref, slot_mate, cosine, sine)
    along_other, sea_other, damp_other = source_state(total_ref, slot_other, cosine, sine)
    own = own_column(total_ref, odd, cosine, sine)
    flow_x = flow_of(total_ref, SUM_X, 1 + odd)
    sign = jnp.where(odd > 0, 1.0, -1.0)
    face_mate = (0.5 * sign) * (flow_x + flow_of(total_ref, SUM_X, slot_mate))
    face_other = (-0.5 * sign) * (flow_x + flow_of(total_ref, SUM_X, slot_other))
    face_mate = jnp.broadcast_to(face_mate, lanes)
    face_other = jnp.broadcast_to(face_other, lanes)
    signed_cosine = [sign * cosine[k] for k in range(4)]

    def level(base, frequency, speed, sums):
        square = frequency * frequency
        scale = own["sea"] / (1.0 + square * own["damp"])
        scale_mate = sea_mate / (1.0 + square * damp_mate)
        scale_other = sea_other / (1.0 + square * damp_other)
        for k in range(4):
            at = pl.ds(pl.multiple_of(base + 8 * k, 8), 8)
            mate = forced_of(mate_ref[at, :], scale_mate, frequency, along_mate[k])
            other = forced_of(other_ref[at, :], scale_other, frequency, along_other[k])
            speed_x = speed * signed_cosine[k]
            mate = jnp.maximum(face_mate + speed_x, 0.0) * mate
            other = jnp.maximum(face_other - speed_x, 0.0) * other
            keep, _, _ = kept_and_sent(own, own_ref[at, :], scale, frequency, speed, k)
            updated_ref[at, :] = (keep + (mate + other)) * own["sea"]
        return sums

    over_levels(bins, level, ())


def pick_kernel(columns, coupling_ref, total_ref, out_ref, before_ref, after_ref, cells_ref):
    width = out_ref.shape[1]
    first, _, group = place()
    ocean = jnp.where(group > 0, 1.0, 0.0)
    kept, low, high = 0, 2 * SLOTS, 4 * SLOTS

    def comp(ref, field, index, slot):
        start = field + index * SLOTS + slot
        return ref[start : start + 1, :]

    rows = []
    for index in range(2):
        rows += [
            comp(before_ref, kept, index, 2) + comp(before_ref, high, index, 1) + comp(out_ref, low, index, 1),
            comp(out_ref, kept, index, 1) + comp(before_ref, high, index, 2) + comp(out_ref, low, index, 2),
            comp(out_ref, kept, index, 2) + comp(out_ref, high, index, 1) + comp(after_ref, low, index, 1),
            comp(after_ref, kept, index, 1) + comp(out_ref, high, index, 2) + comp(after_ref, low, index, 2),
        ]
    sea = total_ref[SEA * SLOTS : (SEA + 1) * SLOTS, :] * ocean
    drift = jnp.concatenate(rows, axis=0) * jnp.concatenate([sea, sea], axis=0)
    for start in range(0, coupling_ref.shape[1], width):
        part = pl.ds(start, width)
        row, slot = slots_of(coupling_ref[:, part], width, first, columns)
        value = jnp.take_along_axis(drift, jnp.broadcast_to(row, drift.shape), axis=1)
        picked = []
        for index in range(2):
            base = index * SLOTS
            picked.append(
                jnp.where(
                    slot < 2,
                    jnp.where(slot < 1, value[base : base + 1], value[base + 1 : base + 2]),
                    jnp.where(slot < 3, value[base + 2 : base + 3], value[base + 3 : base + 4]),
                )
            )
        cells_ref[0:1, part] = picked[0]
        cells_ref[1:2, part] = picked[1]


def direction_table(width):
    heading = np.arange(NDIR) * (2.0 * math.pi / NDIR)
    table = np.concatenate([np.cos(heading), np.sin(heading)]).astype(np.float32)
    return jnp.asarray(np.repeat(table[:, None], width, axis=1))


def body(spectrum, sea_mask, wind, currents, coupling):
    bins, _, width = spectrum.shape
    cells = coupling.shape[1]
    devices = lax.axis_size("dev")
    groups = lax.axis_size("grp")
    mates = [(i, i ^ 1) for i in range(devices)]
    others = [(i, (i + (1 if i % 2 else -1)) % devices) for i in range(devices)]

    def crossed(value, group_step, chip_step):
        def target(group, dev):
            if groups & (groups - 1):
                group = (group + group_step) % groups
            else:
                group = group ^ group_step
            return group * devices + ((dev + 2 * chip_step) % devices ^ 1)

        pairs = [(g * devices + d, target(g, d)) for g in range(groups) for d in range(devices)]
        return lax.ppermute(value, ("grp", "dev"), pairs)

    own = spectrum.reshape(bins, width)
    mate = lax.ppermute(own, "dev", mates)
    other = lax.ppermute(own, "dev", others)

    anywhere = pl.BlockSpec(memory_space=pl.ANY)
    band = pl.pallas_call(
        functools.partial(band_kernel, devices),
        out_shape=pltpu.VMEM((FIELDS * SLOTS, width), jnp.float32),
        in_specs=[anywhere] * 5,
        out_specs=VMEM,
        scratch_shapes=[
            pltpu.VMEM((1, cells), jnp.int32),
            pltpu.VMEM((2, cells), jnp.float32),
            pltpu.VMEM((bins, width), jnp.float32),
            pltpu.VMEM((1, width), jnp.int32),
            pltpu.VMEM((2, width), jnp.float32),
            pltpu.SemaphoreType.DMA((5,)),
        ],
    )(coupling, currents[0], own, sea_mask, wind[:, 0])
    band = band + lax.ppermute(band, "dev", mates)
    parts = [crossed(band, step, 0) for step in range(1, groups)]
    for part in parts:
        band = band + part
    before = crossed(band, 0, 1)
    after = crossed(band, 0, -1)

    table = direction_table(width)
    out, total = pl.pallas_call(
        home_kernel,
        out_shape=(
            pltpu.VMEM((6 * SLOTS, width), jnp.float32),
            pltpu.VMEM((FIELDS * SLOTS, width), jnp.float32),
        ),
        in_specs=[VMEM] * 6,
        out_specs=(VMEM,) * 2,
    )(*near(table, own, mate, band, before, after))
    out = out + lax.ppermute(out, "dev", mates)
    out_before = crossed(out, 0, 1)
    out_after = crossed(out, 0, -1)
    updated = pl.pallas_call(
        update_kernel,
        out_shape=pltpu.VMEM((bins, width), jnp.float32),
        in_specs=[VMEM] * 5,
        out_specs=VMEM,
    )(*near(table, own, mate, other, total))
    cell_drift = pl.pallas_call(
        functools.partial(pick_kernel, devices),
        out_shape=jax.ShapeDtypeStruct(currents.shape[1:], jnp.float32),
        in_specs=[VMEM] * 5,
        out_specs=VMEM,
    )(*near(coupling, total, out, out_before, out_after))
    return updated.reshape(spectrum.shape), cell_drift[None]


def solution(mesh):
    return jax.shard_map(
        body,
        mesh=mesh,
        in_specs=(
            P(None, "dev", None),
            P("dev", None),
            P(None, "dev", None),
            P("grp", None, "dev"),
            P("grp", "dev"),
        ),
        out_specs=(P(None, "dev", None), P("grp", None, "dev")),
        check_vma=False,
    )
```

```python
import functools
import math

import jax
import jax.numpy as jnp
import numpy as np
from jax import lax
from jax.experimental import pallas as pl
from jax.experimental.pallas import tpu as pltpu
from jax.sharding import PartitionSpec as P

NDIR = 32
FIRST_FREQ = 0.04
GROWTH = 1.1
SPEED_TOP = 0.45
CURRENT_TOP = 0.2
WIND_GAIN = 0.03
WHITECAP = 0.3
STEEP_SCALE = 0.4
STOKES_GAIN = 3.0

SLOTS = 4
FIELDS = 8
SUM_X, SUM_Y, COUNT, SEA, WIND_X, WIND_Y, DAMP = range(7)
VMEM = pl.BlockSpec(memory_space=pltpu.VMEM)


def near(*arrays):
    return [pltpu.with_memory_space_constraint(array, pltpu.VMEM) for array in arrays]


def place():
    me = lax.axis_index("dev")
    odd = lax.rem(me, 2)
    return me - odd - 1, odd, lax.axis_index("grp")


def level_groups(levels):
    for size in (12, 6, 4, 3, 2):
        if levels % size == 0:
            return levels // size, size
    return levels, 1


def slots_of(coupling, width, first, columns):
    col = lax.div(coupling, jnp.int32(width))
    row = coupling - col * width
    slot = col - first
    slot = jnp.where(slot < 0, slot + columns, slot)
    slot = jnp.where(slot >= columns, slot - columns, slot)
    return row, slot


def band_kernel(
    columns, coupling_hbm, currents_hbm, spectrum_ref, sea_hbm, wind_hbm, band_ref,
    coupling_ref, currents_ref, sea_ref, wind_ref, sems,
):
    bins, width = spectrum_ref.shape
    first, odd, group = place()
    is_ocean = group > 0

    @pl.when(is_ocean)
    def _():
        copies = [
            pltpu.make_async_copy(coupling_hbm, coupling_ref, sems.at[0]),
            pltpu.make_async_copy(currents_hbm, currents_ref, sems.at[1]),
        ]
        for copy in copies:
            copy.start()
        for copy in copies:
            copy.wait()
        row, slot = slots_of(coupling_ref[...], width, first, columns)
        cells = row.shape[1]
        parts_x, parts_y = [], []
        for comp, parts in ((0, parts_x), (1, parts_y)):
            rest = currents_ref[comp : comp + 1, :]
            for _ in range(3):
                part = rest.astype(jnp.bfloat16).astype(jnp.float32)
                parts.append(part)
                rest = rest - part
        slot_id = lax.broadcasted_iota(jnp.int32, (SLOTS, cells), 0)
        here = jnp.where(slot_id == slot, 1.0, 0.0)
        rows = []
        for part in range(3):
            rows += [here * parts_x[part], here * parts_y[part]]
        rows += [here, jnp.zeros_like(here)]
        values = jnp.concatenate(rows, axis=0).astype(jnp.bfloat16)
        row_id = lax.broadcasted_iota(jnp.int32, (width, cells), 0)
        hot = jnp.where(row_id == row, 1.0, 0.0).astype(jnp.bfloat16)
        sums = lax.dot_general(
            values, hot, (((1,), (1,)), ((), ())), preferred_element_type=jnp.float32
        )
        step = 2 * SLOTS
        band_ref[0:step, :] = sums[0:step] + sums[step : 2 * step] + sums[2 * step : 3 * step]
        band_ref[step : 2 * step, :] = sums[3 * step : 4 * step]
        band_ref[2 * step : 4 * step, :] = jnp.zeros((2 * step, width), jnp.float32)

    @pl.when(jnp.logical_not(is_ocean))
    def _():
        copies = [
            pltpu.make_async_copy(sea_hbm, sea_ref, sems.at[2]),
            pltpu.make_async_copy(wind_hbm, wind_ref, sems.at[3]),
        ]
        for copy in copies:
            copy.start()
        band_ref[...] = jnp.zeros_like(band_ref)
        total = jnp.zeros((8, width), jnp.float32)
        moment = jnp.zeros((8, width), jnp.float32)
        for level in range(bins // NDIR):
            frequency = FIRST_FREQ * GROWTH**level
            block = spectrum_ref[level * NDIR : (level + 1) * NDIR, :]
            block = block[0:8] + block[8:16] + (block[16:24] + block[24:32])
            total += (0.1 * frequency) * block
            moment += (0.1 * frequency * frequency) * block
        for copy in copies:
            copy.wait()
        sea = sea_ref[...].astype(jnp.float32)
        total = jnp.sum(total, axis=0, keepdims=True) * sea
        moment = jnp.sum(moment, axis=0, keepdims=True) * sea
        is_sea = sea > 0.5
        mean_freq = jnp.where(is_sea, moment / jnp.where(is_sea, total, 1.0), 1.0)
        square = mean_freq * mean_freq
        steep = STEEP_SCALE * total * (square * square)
        damp = WHITECAP * (steep * steep) / square
        own = odd + 1
        band_ref[pl.ds(SEA * SLOTS + own, 1), :] = sea
        band_ref[pl.ds(WIND_X * SLOTS + own, 1), :] = wind_ref[0:1, :]
        band_ref[pl.ds(WIND_Y * SLOTS + own, 1), :] = wind_ref[1:2, :]
        band_ref[pl.ds(DAMP * SLOTS + own, 1), :] = damp


def step_kernel(
    table_ref, own_ref, mate_ref, other_ref, band_ref, before_ref, after_ref, updated_ref, drift_ref
):
    bins, width = own_ref.shape
    lanes = 8
    outer_count, inner_count = level_groups(bins // NDIR)
    _, odd, _ = place()
    slot_own, slot_mate, slot_other = 1 + odd, 2 - odd, 3 * odd

    def field(index, slot):
        base = index * SLOTS
        value = band_ref[pl.ds(base + slot, 1), :]
        low = before_ref[pl.ds(base + jnp.minimum(slot, 1) + 2, 1), :]
        high = after_ref[pl.ds(base + jnp.maximum(slot, 2) - 2, 1), :]
        return value + jnp.where(slot < 2, low, high)

    cosine = [table_ref[8 * k : 8 * k + 8, :] for k in range(4)]
    sine = [table_ref[NDIR + 8 * k : NDIR + 8 * k + 8, :] for k in range(4)]

    def column_state(slot):
        count = jnp.maximum(field(COUNT, slot), 1.0)
        mean_x = field(SUM_X, slot) / count
        mean_y = field(SUM_Y, slot) / count
        rel_x = field(WIND_X, slot) - mean_x
        rel_y = field(WIND_Y, slot) - mean_y
        gain = WIND_GAIN * 0.64
        along = [(gain * rel_x) * cosine[k] + (gain * rel_y) * sine[k] for k in range(4)]
        sea = jnp.broadcast_to(field(SEA, slot), (lanes, width))
        damp = jnp.broadcast_to(field(DAMP, slot), (lanes, width))
        return mean_x, mean_y, along, sea, damp

    own_x, own_y, along_own, sea_own, damp_own = column_state(slot_own)
    mate_x, _, along_mate, sea_mate, damp_mate = column_state(slot_mate)
    other_x, _, along_other, sea_other, damp_other = column_state(slot_other)
    flow_x = CURRENT_TOP * jnp.tanh(own_x)
    flow_y = CURRENT_TOP * jnp.tanh(own_y)
    sign = jnp.where(odd > 0, 1.0, -1.0)
    face_mate = jnp.broadcast_to(
        (0.5 * sign) * (flow_x + CURRENT_TOP * jnp.tanh(mate_x)), (lanes, width)
    )
    face_other = jnp.broadcast_to(
        (-0.5 * sign) * (flow_x + CURRENT_TOP * jnp.tanh(other_x)), (lanes, width)
    )
    flow_y = jnp.broadcast_to(flow_y, (lanes, width))
    face_north = 0.5 * (flow_y + pltpu.roll(flow_y, width - 1, 1))
    inner = jnp.where(
        lax.broadcasted_iota(jnp.int32, (lanes, width), 1) < width - 1, 1.0, 0.0
    )
    signed_cosine = [sign * cosine[k] for k in range(4)]

    def level_step(index, carry):
        frequency, speed, sums = carry
        sums = list(sums)
        for sub in range(inner_count):
            square = frequency * frequency
            scale_own = sea_own / (1.0 + square * damp_own)
            scale_mate = sea_mate / (1.0 + square * damp_mate)
            scale_other = sea_other / (1.0 + square * damp_other)
            weight = (STOKES_GAIN * 0.1) * (square * square)
            base = (index * inner_count + sub) * NDIR
            for k in range(4):
                rows = pl.ds(pl.multiple_of(base + 8 * k, 8), 8)

                def forced_of(ref, scale, along):
                    grown = jnp.maximum(frequency * along[k] + (1.0 - WIND_GAIN), 1.0)
                    return (ref[rows, :] * scale) * grown

                forced = forced_of(own_ref, scale_own, along_own)
                forced_mate = forced_of(mate_ref, scale_mate, along_mate)
                forced_other = forced_of(other_ref, scale_other, along_other)
                speed_x = speed * signed_cosine[k]
                q_mate = face_mate + speed_x
                q_other = face_other - speed_x
                in_mate = jnp.maximum(q_mate, 0.0)
                in_other = jnp.maximum(q_other, 0.0)
                out = (in_mate - q_mate) + (in_other - q_other)
                north = speed * sine[k] + face_north
                flux = (
                    jnp.maximum(north, 0.0) * forced
                    + jnp.minimum(north, 0.0) * pltpu.roll(forced, width - 1, 1)
                ) * inner
                new = forced - out * forced + (in_mate * forced_mate + in_other * forced_other)
                new = (new - (flux - pltpu.roll(flux, 1, 1))) * sea_own
                updated_ref[rows, :] = new
                sums[k] = sums[k] + weight * new
            frequency = frequency * GROWTH
            speed = speed * (1.0 / GROWTH)
        return frequency, speed, tuple(sums)

    zero = jnp.zeros((lanes, width), jnp.float32)
    start = (jnp.float32(FIRST_FREQ), jnp.float32(SPEED_TOP), (zero,) * 4)
    _, _, sums = lax.fori_loop(0, outer_count, level_step, start)
    drift_x = sums[0] * cosine[0]
    drift_y = sums[0] * sine[0]
    for k in range(1, 4):
        drift_x = drift_x + sums[k] * cosine[k]
        drift_y = drift_y + sums[k] * sine[k]
    drift_ref[0:1, :] = jnp.sum(drift_x, axis=0, keepdims=True)
    drift_ref[1:2, :] = jnp.sum(drift_y, axis=0, keepdims=True)
    drift_ref[2:8, :] = jnp.zeros((6, width), jnp.float32)


def pick_kernel(columns, coupling_ref, own_ref, mate_ref, other_ref, cells_ref):
    width = own_ref.shape[1]
    first, odd, group = place()
    ocean = jnp.where(group > 0, 1.0, 0.0)
    for start in range(0, coupling_ref.shape[1], width):
        part = pl.ds(start, width)
        row, slot = slots_of(coupling_ref[:, part], width, first, columns)
        row = jnp.broadcast_to(row, (8, width))
        own = jnp.take_along_axis(own_ref[...], row, axis=1)[0:2]
        mate = jnp.take_along_axis(mate_ref[...], row, axis=1)[0:2]
        other = jnp.take_along_axis(other_ref[...], row, axis=1)[0:2]
        value = jnp.where(slot == 1 + odd, own, jnp.where(slot == 2 - odd, mate, other))
        cells_ref[:, part] = value * ocean


def direction_table(width):
    heading = np.arange(NDIR) * (2.0 * math.pi / NDIR)
    table = np.concatenate([np.cos(heading), np.sin(heading)]).astype(np.float32)
    return jnp.asarray(np.repeat(table[:, None], width, axis=1))


def body(spectrum, sea_mask, wind, currents, coupling):
    bins, _, width = spectrum.shape
    devices = lax.axis_size("dev")
    groups = lax.axis_size("grp")
    cells = coupling.shape[1]
    mates = [(i, i ^ 1) for i in range(devices)]
    others = [(i, (i + (1 if i % 2 else -1)) % devices) for i in range(devices)]

    def crossed(value, group_step, chip_step):
        def target(group, dev):
            if groups & (groups - 1):
                group = (group + group_step) % groups
            else:
                group = group ^ group_step
            return group * devices + ((dev + 2 * chip_step) % devices ^ 1)

        pairs = [(g * devices + d, target(g, d)) for g in range(groups) for d in range(devices)]
        return lax.ppermute(value, ("grp", "dev"), pairs)

    own = spectrum.reshape(bins, width)
    mate = lax.ppermute(own, "dev", mates)
    other = lax.ppermute(own, "dev", others)

    anywhere = pl.BlockSpec(memory_space=pl.ANY)
    band = pl.pallas_call(
        functools.partial(band_kernel, devices),
        out_shape=pltpu.VMEM((FIELDS * SLOTS, width), jnp.float32),
        in_specs=[anywhere, anywhere, VMEM, anywhere, anywhere],
        out_specs=VMEM,
        scratch_shapes=[
            pltpu.VMEM((1, cells), jnp.int32),
            pltpu.VMEM((2, cells), jnp.float32),
            pltpu.VMEM((1, width), jnp.int32),
            pltpu.VMEM((2, width), jnp.float32),
            pltpu.SemaphoreType.DMA((4,)),
        ],
    )(coupling, currents[0], *near(own), sea_mask, wind[:, 0])
    band = band + lax.ppermute(band, "dev", mates)
    band, mate = lax.optimization_barrier((band, mate))
    parts = [crossed(band, step, 0) for step in range(1, groups)]
    for part in parts:
        band = band + part
    before = crossed(band, 0, 1)
    after = crossed(band, 0, -1)

    updated, drift = pl.pallas_call(
        step_kernel,
        out_shape=(
            pltpu.VMEM((bins, width), jnp.float32),
            pltpu.VMEM((8, width), jnp.float32),
        ),
        in_specs=[VMEM] * 7,
        out_specs=(VMEM, VMEM),
    )(*near(direction_table(width), own, mate, other, band, before, after))

    drift_other = lax.ppermute(drift, "dev", others)
    drift_mate = lax.ppermute(drift, "dev", mates)
    cell_drift = pl.pallas_call(
        functools.partial(pick_kernel, devices),
        out_shape=jax.ShapeDtypeStruct(currents.shape[1:], jnp.float32),
        in_specs=[VMEM] * 4,
        out_specs=VMEM,
    )(*near(coupling, drift, drift_mate, drift_other))
    return updated.reshape(spectrum.shape), cell_drift[None]


def solution(mesh):
    return jax.shard_map(
        body,
        mesh=mesh,
        in_specs=(
            P(None, "dev", None),
            P("dev", None),
            P(None, "dev", None),
            P("grp", None, "dev"),
            P("grp", "dev"),
        ),
        out_specs=(P(None, "dev", None), P("grp", None, "dev")),
        check_vma=False,
    )
```

```python
import functools
import math

import jax
import jax.numpy as jnp
import numpy as np
from jax import lax
from jax.experimental import pallas as pl
from jax.experimental.pallas import tpu as pltpu
from jax.sharding import PartitionSpec as P

NDIR = 32
FIRST_FREQ = 0.04
GROWTH = 1.1
SPEED_TOP = 0.45
CURRENT_TOP = 0.2
WIND_GAIN = 0.03
WHITECAP = 0.3
STEEP_SCALE = 0.4
STOKES_GAIN = 3.0

SLOTS = 4
FIELDS = 8
SUM_X, SUM_Y, COUNT, SEA, WIND_X, WIND_Y, DAMP = range(7)
VMEM = pl.BlockSpec(memory_space=pltpu.VMEM)


def near(*arrays):
    return [pltpu.with_memory_space_constraint(array, pltpu.VMEM) for array in arrays]


def place():
    me = lax.axis_index("dev")
    odd = lax.rem(me, 2)
    return me - odd - 1, odd, lax.axis_index("grp")


def level_groups(levels):
    for size in (12, 6, 4, 3, 2):
        if levels % size == 0:
            return levels // size, size
    return levels, 1


def slots_of(coupling, width, first, columns):
    col = lax.div(coupling, jnp.int32(width))
    row = coupling - col * width
    slot = col - first
    slot = jnp.where(slot < 0, slot + columns, slot)
    slot = jnp.where(slot >= columns, slot - columns, slot)
    return row, slot


def band_kernel(
    columns, coupling_hbm, currents_hbm, spectrum_hbm, sea_hbm, wind_hbm, band_ref, spectrum_ref,
    coupling_ref, currents_ref, sea_ref, wind_ref, sems,
):
    bins, width = spectrum_ref.shape
    first, odd, group = place()
    is_ocean = group > 0
    fetch = pltpu.make_async_copy(spectrum_hbm, spectrum_ref, sems.at[4])
    fetch.start()

    @pl.when(is_ocean)
    def _():
        copies = [
            pltpu.make_async_copy(coupling_hbm, coupling_ref, sems.at[0]),
            pltpu.make_async_copy(currents_hbm, currents_ref, sems.at[1]),
        ]
        for copy in copies:
            copy.start()
        for copy in copies:
            copy.wait()
        row, slot = slots_of(coupling_ref[...], width, first, columns)
        cells = row.shape[1]
        parts_x, parts_y = [], []
        for comp, parts in ((0, parts_x), (1, parts_y)):
            rest = currents_ref[comp : comp + 1, :]
            for _ in range(3):
                part = rest.astype(jnp.bfloat16).astype(jnp.float32)
                parts.append(part)
                rest = rest - part
        slot_id = lax.broadcasted_iota(jnp.int32, (SLOTS, cells), 0)
        here = jnp.where(slot_id == slot, 1.0, 0.0)
        rows = []
        for part in range(3):
            rows += [here * parts_x[part], here * parts_y[part]]
        rows += [here, jnp.zeros_like(here)]
        values = jnp.concatenate(rows, axis=0).astype(jnp.bfloat16)
        row_id = lax.broadcasted_iota(jnp.int32, (width, cells), 0)
        hot = jnp.where(row_id == row, 1.0, 0.0).astype(jnp.bfloat16)
        sums = lax.dot_general(
            values, hot, (((1,), (1,)), ((), ())), preferred_element_type=jnp.float32
        )
        step = 2 * SLOTS
        band_ref[0:step, :] = sums[0:step] + sums[step : 2 * step] + sums[2 * step : 3 * step]
        band_ref[step : 2 * step, :] = sums[3 * step : 4 * step]
        band_ref[2 * step : 4 * step, :] = jnp.zeros((2 * step, width), jnp.float32)
        fetch.wait()

    @pl.when(jnp.logical_not(is_ocean))
    def _():
        copies = [
            pltpu.make_async_copy(sea_hbm, sea_ref, sems.at[2]),
            pltpu.make_async_copy(wind_hbm, wind_ref, sems.at[3]),
        ]
        for copy in copies:
            copy.start()
        band_ref[...] = jnp.zeros_like(band_ref)
        fetch.wait()
        total = jnp.zeros((8, width), jnp.float32)
        moment = jnp.zeros((8, width), jnp.float32)
        for level in range(bins // NDIR):
            frequency = FIRST_FREQ * GROWTH**level
            block = spectrum_ref[level * NDIR : (level + 1) * NDIR, :]
            block = block[0:8] + block[8:16] + (block[16:24] + block[24:32])
            total += (0.1 * frequency) * block
            moment += (0.1 * frequency * frequency) * block
        for copy in copies:
            copy.wait()
        sea = sea_ref[...].astype(jnp.float32)
        total = jnp.sum(total, axis=0, keepdims=True) * sea
        moment = jnp.sum(moment, axis=0, keepdims=True) * sea
        is_sea = sea > 0.5
        mean_freq = jnp.where(is_sea, moment / jnp.where(is_sea, total, 1.0), 1.0)
        square = mean_freq * mean_freq
        steep = STEEP_SCALE * total * (square * square)
        damp = WHITECAP * (steep * steep) / square
        own = odd + 1
        band_ref[pl.ds(SEA * SLOTS + own, 1), :] = sea
        band_ref[pl.ds(WIND_X * SLOTS + own, 1), :] = wind_ref[0:1, :]
        band_ref[pl.ds(WIND_Y * SLOTS + own, 1), :] = wind_ref[1:2, :]
        band_ref[pl.ds(DAMP * SLOTS + own, 1), :] = damp


def step_kernel(
    table_ref, own_ref, mate_ref, other_ref, band_ref, before_ref, after_ref, updated_ref, drift_ref
):
    bins, width = own_ref.shape
    lanes = 8
    outer_count, inner_count = level_groups(bins // NDIR)
    _, odd, _ = place()
    slot_own, slot_mate, slot_other = 1 + odd, 2 - odd, 3 * odd

    def field(index, slot):
        base = index * SLOTS
        value = band_ref[pl.ds(base + slot, 1), :]
        low = before_ref[pl.ds(base + jnp.minimum(slot, 1) + 2, 1), :]
        high = after_ref[pl.ds(base + jnp.maximum(slot, 2) - 2, 1), :]
        return value + jnp.where(slot < 2, low, high)

    cosine = [table_ref[8 * k : 8 * k + 8, :] for k in range(4)]
    sine = [table_ref[NDIR + 8 * k : NDIR + 8 * k + 8, :] for k in range(4)]

    def column_state(slot):
        count = jnp.maximum(field(COUNT, slot), 1.0)
        mean_x = field(SUM_X, slot) / count
        mean_y = field(SUM_Y, slot) / count
        rel_x = field(WIND_X, slot) - mean_x
        rel_y = field(WIND_Y, slot) - mean_y
        gain = WIND_GAIN * 0.64
        along = [(gain * rel_x) * cosine[k] + (gain * rel_y) * sine[k] for k in range(4)]
        sea = jnp.broadcast_to(field(SEA, slot), (lanes, width))
        damp = jnp.broadcast_to(field(DAMP, slot), (lanes, width))
        return mean_x, mean_y, along, sea, damp

    own_x, own_y, along_own, sea_own, damp_own = column_state(slot_own)
    mate_x, _, along_mate, sea_mate, damp_mate = column_state(slot_mate)
    other_x, _, along_other, sea_other, damp_other = column_state(slot_other)
    flow_x = CURRENT_TOP * jnp.tanh(own_x)
    flow_y = CURRENT_TOP * jnp.tanh(own_y)
    sign = jnp.where(odd > 0, 1.0, -1.0)
    face_mate = jnp.broadcast_to(
        (0.5 * sign) * (flow_x + CURRENT_TOP * jnp.tanh(mate_x)), (lanes, width)
    )
    face_other = jnp.broadcast_to(
        (-0.5 * sign) * (flow_x + CURRENT_TOP * jnp.tanh(other_x)), (lanes, width)
    )
    flow_y = jnp.broadcast_to(flow_y, (lanes, width))
    face_north = 0.5 * (flow_y + pltpu.roll(flow_y, width - 1, 1))
    inner = jnp.where(
        lax.broadcasted_iota(jnp.int32, (lanes, width), 1) < width - 1, 1.0, 0.0
    )
    signed_cosine = [sign * cosine[k] for k in range(4)]

    def level_step(index, carry):
        frequency, speed, sums = carry
        sums = list(sums)
        for sub in range(inner_count):
            square = frequency * frequency
            scale_own = sea_own / (1.0 + square * damp_own)
            scale_mate = sea_mate / (1.0 + square * damp_mate)
            scale_other = sea_other / (1.0 + square * damp_other)
            weight = (STOKES_GAIN * 0.1) * (square * square)
            base = (index * inner_count + sub) * NDIR
            for k in range(4):
                rows = pl.ds(pl.multiple_of(base + 8 * k, 8), 8)

                def forced_of(ref, scale, along):
                    grown = jnp.maximum(frequency * along[k] + (1.0 - WIND_GAIN), 1.0)
                    return (ref[rows, :] * scale) * grown

                forced = forced_of(own_ref, scale_own, along_own)
                forced_mate = forced_of(mate_ref, scale_mate, along_mate)
                forced_other = forced_of(other_ref, scale_other, along_other)
                speed_x = speed * signed_cosine[k]
                q_mate = face_mate + speed_x
                q_other = face_other - speed_x
                in_mate = jnp.maximum(q_mate, 0.0)
                in_other = jnp.maximum(q_other, 0.0)
                out = (in_mate - q_mate) + (in_other - q_other)
                north = speed * sine[k] + face_north
                flux = (
                    jnp.maximum(north, 0.0) * forced
                    + jnp.minimum(north, 0.0) * pltpu.roll(forced, width - 1, 1)
                ) * inner
                new = forced - out * forced + (in_mate * forced_mate + in_other * forced_other)
                new = (new - (flux - pltpu.roll(flux, 1, 1))) * sea_own
                updated_ref[rows, :] = new
                sums[k] = sums[k] + weight * new
            frequency = frequency * GROWTH
            speed = speed * (1.0 / GROWTH)
        return frequency, speed, tuple(sums)

    zero = jnp.zeros((lanes, width), jnp.float32)
    start = (jnp.float32(FIRST_FREQ), jnp.float32(SPEED_TOP), (zero,) * 4)
    _, _, sums = lax.fori_loop(0, outer_count, level_step, start)
    drift_x = sums[0] * cosine[0]
    drift_y = sums[0] * sine[0]
    for k in range(1, 4):
        drift_x = drift_x + sums[k] * cosine[k]
        drift_y = drift_y + sums[k] * sine[k]
    drift_ref[0:1, :] = jnp.sum(drift_x, axis=0, keepdims=True)
    drift_ref[1:2, :] = jnp.sum(drift_y, axis=0, keepdims=True)
    drift_ref[2:8, :] = jnp.zeros((6, width), jnp.float32)


def pick_kernel(columns, coupling_ref, own_ref, mate_ref, other_ref, cells_ref):
    width = own_ref.shape[1]
    first, odd, group = place()
    ocean = jnp.where(group > 0, 1.0, 0.0)
    for start in range(0, coupling_ref.shape[1], width):
        part = pl.ds(start, width)
        row, slot = slots_of(coupling_ref[:, part], width, first, columns)
        row = jnp.broadcast_to(row, (8, width))
        own = jnp.take_along_axis(own_ref[...], row, axis=1)[0:2]
        mate = jnp.take_along_axis(mate_ref[...], row, axis=1)[0:2]
        other = jnp.take_along_axis(other_ref[...], row, axis=1)[0:2]
        value = jnp.where(slot == 1 + odd, own, jnp.where(slot == 2 - odd, mate, other))
        cells_ref[:, part] = value * ocean


def direction_table(width):
    heading = np.arange(NDIR) * (2.0 * math.pi / NDIR)
    table = np.concatenate([np.cos(heading), np.sin(heading)]).astype(np.float32)
    return jnp.asarray(np.repeat(table[:, None], width, axis=1))


def body(spectrum, sea_mask, wind, currents, coupling):
    bins, _, width = spectrum.shape
    devices = lax.axis_size("dev")
    groups = lax.axis_size("grp")
    cells = coupling.shape[1]
    mates = [(i, i ^ 1) for i in range(devices)]
    others = [(i, (i + (1 if i % 2 else -1)) % devices) for i in range(devices)]

    def crossed(value, group_step, chip_step):
        def target(group, dev):
            if groups & (groups - 1):
                group = (group + group_step) % groups
            else:
                group = group ^ group_step
            return group * devices + ((dev + 2 * chip_step) % devices ^ 1)

        pairs = [(g * devices + d, target(g, d)) for g in range(groups) for d in range(devices)]
        return lax.ppermute(value, ("grp", "dev"), pairs)

    own = spectrum.reshape(bins, width)
    mate = lax.ppermute(own, "dev", mates)
    other = lax.ppermute(own, "dev", others)

    anywhere = pl.BlockSpec(memory_space=pl.ANY)
    band, own_near = pl.pallas_call(
        functools.partial(band_kernel, devices),
        out_shape=(
            pltpu.VMEM((FIELDS * SLOTS, width), jnp.float32),
            pltpu.VMEM((bins, width), jnp.float32),
        ),
        in_specs=[anywhere] * 5,
        out_specs=(VMEM, VMEM),
        scratch_shapes=[
            pltpu.VMEM((1, cells), jnp.int32),
            pltpu.VMEM((2, cells), jnp.float32),
            pltpu.VMEM((1, width), jnp.int32),
            pltpu.VMEM((2, width), jnp.float32),
            pltpu.SemaphoreType.DMA((5,)),
        ],
    )(coupling, currents[0], own, sea_mask, wind[:, 0])
    band = band + lax.ppermute(band, "dev", mates)
    band, mate = lax.optimization_barrier((band, mate))
    parts = [crossed(band, step, 0) for step in range(1, groups)]
    for part in parts:
        band = band + part
    before = crossed(band, 0, 1)
    after = crossed(band, 0, -1)

    updated, drift = pl.pallas_call(
        step_kernel,
        out_shape=(
            pltpu.VMEM((bins, width), jnp.float32),
            pltpu.VMEM((8, width), jnp.float32),
        ),
        in_specs=[VMEM] * 7,
        out_specs=(VMEM, VMEM),
    )(*near(direction_table(width), own_near, mate, other, band, before, after))

    drift_other = lax.ppermute(drift, "dev", others)
    drift_mate = lax.ppermute(drift, "dev", mates)
    cell_drift = pl.pallas_call(
        functools.partial(pick_kernel, devices),
        out_shape=jax.ShapeDtypeStruct(currents.shape[1:], jnp.float32),
        in_specs=[VMEM] * 4,
        out_specs=VMEM,
    )(*near(coupling, drift, drift_mate, drift_other))
    return updated.reshape(spectrum.shape), cell_drift[None]


def solution(mesh):
    return jax.shard_map(
        body,
        mesh=mesh,
        in_specs=(
            P(None, "dev", None),
            P("dev", None),
            P(None, "dev", None),
            P("grp", None, "dev"),
            P("grp", "dev"),
        ),
        out_specs=(P(None, "dev", None), P("grp", None, "dev")),
        check_vma=False,
    )
```

```python
import functools
import math

import jax
import jax.numpy as jnp
import numpy as np
from jax import lax
from jax.experimental import pallas as pl
from jax.experimental.pallas import tpu as pltpu
from jax.sharding import PartitionSpec as P

NDIR = 32
FIRST_FREQ = 0.04
GROWTH = 1.1
SPEED_TOP = 0.45
CURRENT_TOP = 0.2
WIND_GAIN = 0.03
WHITECAP = 0.3
STEEP_SCALE = 0.4
STOKES_GAIN = 3.0

SLOTS = 4
FIELDS = 6
SUM_X, SUM_Y, COUNT, SEA, WIND_X, WIND_Y = range(FIELDS)
VMEM = pl.BlockSpec(memory_space=pltpu.VMEM)


def near(*arrays):
    return [pltpu.with_memory_space_constraint(array, pltpu.VMEM) for array in arrays]


def place():
    me = lax.axis_index("dev")
    odd = lax.rem(me, 2)
    return me - odd - 1, odd, lax.axis_index("grp")


def level_groups(levels):
    for size in (36, 18, 12, 6, 4, 3, 2):
        if levels % size == 0:
            return levels // size, size
    return levels, 1


def slots_of(coupling, width, first, columns):
    col = lax.div(coupling, jnp.int32(width))
    row = coupling - col * width
    slot = col - first
    slot = jnp.where(slot < 0, slot + columns, slot)
    slot = jnp.where(slot >= columns, slot - columns, slot)
    return row, slot


def band_kernel(
    columns, coupling_hbm, currents_hbm, sea_hbm, wind_hbm, band_ref,
    coupling_ref, currents_ref, sea_ref, wind_ref, sems,
):
    width = band_ref.shape[1]
    first, odd, group = place()
    is_ocean = group > 0

    @pl.when(is_ocean)
    def _():
        copies = [
            pltpu.make_async_copy(coupling_hbm, coupling_ref, sems.at[0]),
            pltpu.make_async_copy(currents_hbm, currents_ref, sems.at[1]),
        ]
        for copy in copies:
            copy.start()
        for copy in copies:
            copy.wait()
        row, slot = slots_of(coupling_ref[...], width, first, columns)
        cells = row.shape[1]
        parts_x, parts_y = [], []
        for comp, parts in ((0, parts_x), (1, parts_y)):
            rest = currents_ref[comp : comp + 1, :]
            for _ in range(3):
                part = rest.astype(jnp.bfloat16).astype(jnp.float32)
                parts.append(part)
                rest = rest - part
        slot_id = lax.broadcasted_iota(jnp.int32, (SLOTS, cells), 0)
        here = jnp.where(slot_id == slot, 1.0, 0.0)
        rows = []
        for part in range(3):
            rows += [here * parts_x[part], here * parts_y[part]]
        rows += [here, jnp.zeros_like(here)]
        values = jnp.concatenate(rows, axis=0).astype(jnp.bfloat16)
        row_id = lax.broadcasted_iota(jnp.int32, (width, cells), 0)
        hot = jnp.where(row_id == row, 1.0, 0.0).astype(jnp.bfloat16)
        sums = lax.dot_general(
            values, hot, (((1,), (1,)), ((), ())), preferred_element_type=jnp.float32
        )
        step = 2 * SLOTS
        band_ref[0:step, :] = sums[0:step] + sums[step : 2 * step] + sums[2 * step : 3 * step]
        band_ref[step : 2 * step, :] = sums[3 * step : 4 * step]
        band_ref[2 * step : 3 * step, :] = jnp.zeros((step, width), jnp.float32)

    @pl.when(jnp.logical_not(is_ocean))
    def _():
        copies = [
            pltpu.make_async_copy(sea_hbm, sea_ref, sems.at[2]),
            pltpu.make_async_copy(wind_hbm, wind_ref, sems.at[3]),
        ]
        for copy in copies:
            copy.start()
        band_ref[...] = jnp.zeros_like(band_ref)
        for copy in copies:
            copy.wait()
        own = odd + 1
        band_ref[pl.ds(SEA * SLOTS + own, 1), :] = sea_ref[...].astype(jnp.float32)
        band_ref[pl.ds(WIND_X * SLOTS + own, 1), :] = wind_ref[0:1, :]
        band_ref[pl.ds(WIND_Y * SLOTS + own, 1), :] = wind_ref[1:2, :]


def spectrum_sums(ref, sums_ref, first_row):
    bins, width = ref.shape
    total = jnp.zeros((8, width), jnp.float32)
    moment = jnp.zeros((8, width), jnp.float32)
    for level in range(bins // NDIR):
        frequency = FIRST_FREQ * GROWTH**level
        block = ref[level * NDIR : (level + 1) * NDIR, :]
        block = block[0:8] + block[8:16] + (block[16:24] + block[24:32])
        total += (0.1 * frequency) * block
        moment += (0.1 * frequency * frequency) * block
    sums_ref[first_row : first_row + 1, :] = jnp.sum(total, axis=0, keepdims=True)
    sums_ref[first_row + 1 : first_row + 2, :] = jnp.sum(moment, axis=0, keepdims=True)


def fetch_kernel(own_hbm, _, own_ref, sums_ref, sem):
    fetch = pltpu.make_async_copy(own_hbm, own_ref, sem)
    fetch.start()
    sums_ref[...] = jnp.zeros_like(sums_ref)
    fetch.wait()
    spectrum_sums(own_ref, sums_ref, 0)


def damping_of(sums_ref, place_row, sea):
    total = sums_ref[place_row : place_row + 1, :] * sea
    moment = sums_ref[place_row + 1 : place_row + 2, :] * sea
    is_sea = sea > 0.5
    mean_freq = jnp.where(is_sea, moment / jnp.where(is_sea, total, 1.0), 1.0)
    square = mean_freq * mean_freq
    steep = STEEP_SCALE * total * (square * square)
    return WHITECAP * (steep * steep) / square


def step_kernel(
    table_ref, own_ref, sums_ref, mate_ref, other_ref, band_ref, before_ref, after_ref, updated_ref, drift_ref,
    other_sums_ref,
):
    bins, width = own_ref.shape
    lanes = 8
    spectrum_sums(mate_ref, other_sums_ref, 2)
    spectrum_sums(other_ref, other_sums_ref, 0)
    outer_count, inner_count = level_groups(bins // NDIR)
    _, odd, _ = place()
    slot_own, slot_mate, slot_other = 1 + odd, 2 - odd, 3 * odd

    def field(index, slot):
        base = index * SLOTS
        value = band_ref[pl.ds(base + slot, 1), :]
        low = before_ref[pl.ds(base + jnp.minimum(slot, 1) + 2, 1), :]
        high = after_ref[pl.ds(base + jnp.maximum(slot, 2) - 2, 1), :]
        return value + jnp.where(slot < 2, low, high)

    cosine = [table_ref[8 * k : 8 * k + 8, :] for k in range(4)]
    sine = [table_ref[NDIR + 8 * k : NDIR + 8 * k + 8, :] for k in range(4)]

    def column_state(slot, sums, place_row):
        count = jnp.maximum(field(COUNT, slot), 1.0)
        mean_x = field(SUM_X, slot) / count
        mean_y = field(SUM_Y, slot) / count
        rel_x = field(WIND_X, slot) - mean_x
        rel_y = field(WIND_Y, slot) - mean_y
        gain = WIND_GAIN * 0.64
        along = [(gain * rel_x) * cosine[k] + (gain * rel_y) * sine[k] for k in range(4)]
        sea = field(SEA, slot)
        damp = jnp.broadcast_to(damping_of(sums, place_row, sea), (lanes, width))
        sea = jnp.broadcast_to(sea, (lanes, width))
        return mean_x, mean_y, along, sea, damp

    own_x, own_y, along_own, sea_own, damp_own = column_state(slot_own, sums_ref, 0)
    mate_x, _, along_mate, sea_mate, damp_mate = column_state(slot_mate, other_sums_ref, 2)
    other_x, _, along_other, sea_other, damp_other = column_state(slot_other, other_sums_ref, 0)
    flow_x = CURRENT_TOP * jnp.tanh(own_x)
    flow_y = CURRENT_TOP * jnp.tanh(own_y)
    sign = jnp.where(odd > 0, 1.0, -1.0)
    face_mate = jnp.broadcast_to(
        (0.5 * sign) * (flow_x + CURRENT_TOP * jnp.tanh(mate_x)), (lanes, width)
    )
    face_other = jnp.broadcast_to(
        (-0.5 * sign) * (flow_x + CURRENT_TOP * jnp.tanh(other_x)), (lanes, width)
    )
    flow_y = jnp.broadcast_to(flow_y, (lanes, width))
    face_north = 0.5 * (flow_y + pltpu.roll(flow_y, width - 1, 1))
    inner = jnp.where(
        lax.broadcasted_iota(jnp.int32, (lanes, width), 1) < width - 1, 1.0, 0.0
    )
    signed_cosine = [sign * cosine[k] for k in range(4)]

    def level_step(index, carry):
        frequency, speed, sums = carry
        sums = list(sums)
        for sub in range(inner_count):
            square = frequency * frequency
            scale_own = sea_own / (1.0 + square * damp_own)
            scale_mate = sea_mate / (1.0 + square * damp_mate)
            scale_other = sea_other / (1.0 + square * damp_other)
            weight = (STOKES_GAIN * 0.1) * (square * square)
            base = (index * inner_count + sub) * NDIR
            for k in range(4):
                rows = pl.ds(pl.multiple_of(base + 8 * k, 8), 8)

                def forced_of(ref, scale, along):
                    grown = jnp.maximum(frequency * along[k] + (1.0 - WIND_GAIN), 1.0)
                    return (ref[rows, :] * scale) * grown

                forced = forced_of(own_ref, scale_own, along_own)
                forced_mate = forced_of(mate_ref, scale_mate, along_mate)
                forced_other = forced_of(other_ref, scale_other, along_other)
                speed_x = speed * signed_cosine[k]
                q_mate = face_mate + speed_x
                q_other = face_other - speed_x
                in_mate = jnp.maximum(q_mate, 0.0)
                in_other = jnp.maximum(q_other, 0.0)
                out = (in_mate - q_mate) + (in_other - q_other)
                north = speed * sine[k] + face_north
                flux = (
                    jnp.maximum(north, 0.0) * forced
                    + jnp.minimum(north, 0.0) * pltpu.roll(forced, width - 1, 1)
                ) * inner
                new = forced - out * forced + (in_mate * forced_mate + in_other * forced_other)
                new = (new - (flux - pltpu.roll(flux, 1, 1))) * sea_own
                updated_ref[rows, :] = new
                sums[k] = sums[k] + weight * new
            frequency = frequency * GROWTH
            speed = speed * (1.0 / GROWTH)
        return frequency, speed, tuple(sums)

    zero = jnp.zeros((lanes, width), jnp.float32)
    start = (jnp.float32(FIRST_FREQ), jnp.float32(SPEED_TOP), (zero,) * 4)
    _, _, sums = lax.fori_loop(0, outer_count, level_step, start)
    drift_x = sums[0] * cosine[0]
    drift_y = sums[0] * sine[0]
    for k in range(1, 4):
        drift_x = drift_x + sums[k] * cosine[k]
        drift_y = drift_y + sums[k] * sine[k]
    drift_ref[0:1, :] = jnp.sum(drift_x, axis=0, keepdims=True)
    drift_ref[1:2, :] = jnp.sum(drift_y, axis=0, keepdims=True)
    drift_ref[2:8, :] = jnp.zeros((6, width), jnp.float32)


def pick_kernel(columns, coupling_ref, own_ref, mate_ref, other_ref, cells_ref):
    width = own_ref.shape[1]
    first, odd, group = place()
    ocean = jnp.where(group > 0, 1.0, 0.0)
    for start in range(0, coupling_ref.shape[1], width):
        part = pl.ds(start, width)
        row, slot = slots_of(coupling_ref[:, part], width, first, columns)
        row = jnp.broadcast_to(row, (8, width))
        own = jnp.take_along_axis(own_ref[...], row, axis=1)[0:2]
        mate = jnp.take_along_axis(mate_ref[...], row, axis=1)[0:2]
        other = jnp.take_along_axis(other_ref[...], row, axis=1)[0:2]
        value = jnp.where(slot == 1 + odd, own, jnp.where(slot == 2 - odd, mate, other))
        cells_ref[:, part] = value * ocean


def direction_table(width):
    heading = np.arange(NDIR) * (2.0 * math.pi / NDIR)
    table = np.concatenate([np.cos(heading), np.sin(heading)]).astype(np.float32)
    return jnp.asarray(np.repeat(table[:, None], width, axis=1))


def body(spectrum, sea_mask, wind, currents, coupling):
    bins, _, width = spectrum.shape
    devices = lax.axis_size("dev")
    groups = lax.axis_size("grp")
    cells = coupling.shape[1]
    mates = [(i, i ^ 1) for i in range(devices)]
    others = [(i, (i + (1 if i % 2 else -1)) % devices) for i in range(devices)]

    def crossed(value, group_step, chip_step):
        def target(group, dev):
            if groups & (groups - 1):
                group = (group + group_step) % groups
            else:
                group = group ^ group_step
            return group * devices + ((dev + 2 * chip_step) % devices ^ 1)

        pairs = [(g * devices + d, target(g, d)) for g in range(groups) for d in range(devices)]
        return lax.ppermute(value, ("grp", "dev"), pairs)

    own = spectrum.reshape(bins, width)
    other = lax.ppermute(own, "dev", others)
    mate = lax.ppermute(own, "dev", mates)

    anywhere = pl.BlockSpec(memory_space=pl.ANY)
    band = pl.pallas_call(
        functools.partial(band_kernel, devices),
        out_shape=pltpu.VMEM((FIELDS * SLOTS, width), jnp.float32),
        in_specs=[anywhere] * 4,
        out_specs=VMEM,
        scratch_shapes=[
            pltpu.VMEM((1, cells), jnp.int32),
            pltpu.VMEM((2, cells), jnp.float32),
            pltpu.VMEM((1, width), jnp.int32),
            pltpu.VMEM((2, width), jnp.float32),
            pltpu.SemaphoreType.DMA((4,)),
        ],
    )(coupling, currents[0], sea_mask, wind[:, 0])
    band = band + lax.ppermute(band, "dev", mates)
    parts = [crossed(band, step, 0) for step in range(1, groups)]
    for part in parts:
        band = band + part
    before = crossed(band, 0, 1)
    after = crossed(band, 0, -1)

    own_near, sums = pl.pallas_call(
        fetch_kernel,
        out_shape=(
            pltpu.VMEM((bins, width), jnp.float32),
            pltpu.VMEM((8, width), jnp.float32),
        ),
        in_specs=[anywhere, VMEM],
        out_specs=(VMEM, VMEM),
        scratch_shapes=[pltpu.SemaphoreType.DMA],
    )(own, *near(band))
    updated, drift = pl.pallas_call(
        step_kernel,
        out_shape=(
            pltpu.VMEM((bins, width), jnp.float32),
            pltpu.VMEM((8, width), jnp.float32),
        ),
        in_specs=[VMEM] * 8,
        out_specs=(VMEM, VMEM),
        scratch_shapes=[pltpu.VMEM((8, width), jnp.float32)],
    )(*near(direction_table(width), own_near, sums, mate, other, band, before, after))

    drift_other = lax.ppermute(drift, "dev", others)
    drift_mate = lax.ppermute(drift, "dev", mates)
    cell_drift = pl.pallas_call(
        functools.partial(pick_kernel, devices),
        out_shape=jax.ShapeDtypeStruct(currents.shape[1:], jnp.float32),
        in_specs=[VMEM] * 4,
        out_specs=VMEM,
    )(*near(coupling, drift, drift_mate, drift_other))
    return updated.reshape(spectrum.shape), cell_drift[None]


def solution(mesh):
    return jax.shard_map(
        body,
        mesh=mesh,
        in_specs=(
            P(None, "dev", None),
            P("dev", None),
            P(None, "dev", None),
            P("grp", None, "dev"),
            P("grp", "dev"),
        ),
        out_specs=(P(None, "dev", None), P("grp", None, "dev")),
        check_vma=False,
    )
```

```python
import functools
import math

import jax
import jax.numpy as jnp
import numpy as np
from jax import lax
from jax.experimental import pallas as pl
from jax.experimental.pallas import tpu as pltpu
from jax.sharding import PartitionSpec as P

NDIR = 32
FIRST_FREQ = 0.04
GROWTH = 1.1
SPEED_TOP = 0.45
CURRENT_TOP = 0.2
WIND_GAIN = 0.03
WHITECAP = 0.3
STEEP_SCALE = 0.4
STOKES_GAIN = 3.0

SLOTS = 4
FIELDS = 6
SUM_X, SUM_Y, COUNT, SEA, WIND_X, WIND_Y = range(FIELDS)
VMEM = pl.BlockSpec(memory_space=pltpu.VMEM)


def near(*arrays):
    return [pltpu.with_memory_space_constraint(array, pltpu.VMEM) for array in arrays]


def place():
    me = lax.axis_index("dev")
    odd = lax.rem(me, 2)
    return me - odd - 1, odd, lax.axis_index("grp")


def level_groups(levels):
    for size in (36, 18, 12, 6, 4, 3, 2):
        if levels % size == 0:
            return levels // size, size
    return levels, 1


def slots_of(coupling, width, first, columns):
    col = lax.div(coupling, jnp.int32(width))
    row = coupling - col * width
    slot = col - first
    slot = jnp.where(slot < 0, slot + columns, slot)
    slot = jnp.where(slot >= columns, slot - columns, slot)
    return row, slot


def band_kernel(
    columns, coupling_hbm, currents_hbm, sea_hbm, wind_hbm, band_ref,
    coupling_ref, currents_ref, sea_ref, wind_ref, sems,
):
    width = band_ref.shape[1]
    first, odd, group = place()
    is_ocean = group > 0

    @pl.when(is_ocean)
    def _():
        copies = [
            pltpu.make_async_copy(coupling_hbm, coupling_ref, sems.at[0]),
            pltpu.make_async_copy(currents_hbm, currents_ref, sems.at[1]),
        ]
        for copy in copies:
            copy.start()
        for copy in copies:
            copy.wait()
        row, slot = slots_of(coupling_ref[...], width, first, columns)
        cells = row.shape[1]
        parts_x, parts_y = [], []
        for comp, parts in ((0, parts_x), (1, parts_y)):
            rest = currents_ref[comp : comp + 1, :]
            for _ in range(3):
                part = rest.astype(jnp.bfloat16).astype(jnp.float32)
                parts.append(part)
                rest = rest - part
        slot_id = lax.broadcasted_iota(jnp.int32, (SLOTS, cells), 0)
        here = jnp.where(slot_id == slot, 1.0, 0.0)
        rows = []
        for part in range(3):
            rows += [here * parts_x[part], here * parts_y[part]]
        rows += [here, jnp.zeros_like(here)]
        values = jnp.concatenate(rows, axis=0).astype(jnp.bfloat16)
        row_id = lax.broadcasted_iota(jnp.int32, (width, cells), 0)
        hot = jnp.where(row_id == row, 1.0, 0.0).astype(jnp.bfloat16)
        sums = lax.dot_general(
            values, hot, (((1,), (1,)), ((), ())), preferred_element_type=jnp.float32
        )
        step = 2 * SLOTS
        band_ref[0:step, :] = sums[0:step] + sums[step : 2 * step] + sums[2 * step : 3 * step]
        band_ref[step : 2 * step, :] = sums[3 * step : 4 * step]
        band_ref[2 * step : 3 * step, :] = jnp.zeros((step, width), jnp.float32)

    @pl.when(jnp.logical_not(is_ocean))
    def _():
        copies = [
            pltpu.make_async_copy(sea_hbm, sea_ref, sems.at[2]),
            pltpu.make_async_copy(wind_hbm, wind_ref, sems.at[3]),
        ]
        for copy in copies:
            copy.start()
        band_ref[...] = jnp.zeros_like(band_ref)
        for copy in copies:
            copy.wait()
        own = odd + 1
        band_ref[pl.ds(SEA * SLOTS + own, 1), :] = sea_ref[...].astype(jnp.float32)
        band_ref[pl.ds(WIND_X * SLOTS + own, 1), :] = wind_ref[0:1, :]
        band_ref[pl.ds(WIND_Y * SLOTS + own, 1), :] = wind_ref[1:2, :]


def spectrum_sums(ref, sums_ref, first_row):
    bins, width = ref.shape
    total = jnp.zeros((8, width), jnp.float32)
    moment = jnp.zeros((8, width), jnp.float32)
    for level in range(bins // NDIR):
        frequency = FIRST_FREQ * GROWTH**level
        block = ref[level * NDIR : (level + 1) * NDIR, :]
        block = block[0:8] + block[8:16] + (block[16:24] + block[24:32])
        total += (0.1 * frequency) * block
        moment += (0.1 * frequency * frequency) * block
    sums_ref[first_row : first_row + 1, :] = jnp.sum(total, axis=0, keepdims=True)
    sums_ref[first_row + 1 : first_row + 2, :] = jnp.sum(moment, axis=0, keepdims=True)


def fetch_kernel(own_hbm, _, own_ref, sums_ref, sem):
    fetch = pltpu.make_async_copy(own_hbm, own_ref, sem)
    fetch.start()
    sums_ref[...] = jnp.zeros_like(sums_ref)
    fetch.wait()
    spectrum_sums(own_ref, sums_ref, 0)


def damping_of(sums_ref, place_row, sea):
    total = sums_ref[place_row : place_row + 1, :] * sea
    moment = sums_ref[place_row + 1 : place_row + 2, :] * sea
    is_sea = sea > 0.5
    mean_freq = jnp.where(is_sea, moment / jnp.where(is_sea, total, 1.0), 1.0)
    square = mean_freq * mean_freq
    steep = STEEP_SCALE * total * (square * square)
    return WHITECAP * (steep * steep) / square


def step_kernel(
    table_ref, own_ref, sums_ref, mate_ref, other_ref, band_ref, after_ref, before_ref, updated_ref, drift_ref,
    other_sums_ref,
):
    bins, width = own_ref.shape
    lanes = 8
    spectrum_sums(mate_ref, other_sums_ref, 2)
    spectrum_sums(other_ref, other_sums_ref, 0)
    outer_count, inner_count = level_groups(bins // NDIR)
    _, odd, _ = place()
    slot_own, slot_mate, slot_other = 1 + odd, 2 - odd, 3 * odd

    def field(index, slot):
        base = index * SLOTS
        value = band_ref[pl.ds(base + slot, 1), :]
        low = before_ref[pl.ds(base + jnp.minimum(slot, 1) + 2, 1), :]
        high = after_ref[pl.ds(base + jnp.maximum(slot, 2) - 2, 1), :]
        return value + jnp.where(slot < 2, low, high)

    cosine = [table_ref[8 * k : 8 * k + 8, :] for k in range(4)]
    sine = [table_ref[NDIR + 8 * k : NDIR + 8 * k + 8, :] for k in range(4)]

    def column_state(slot, sums, place_row):
        count = jnp.maximum(field(COUNT, slot), 1.0)
        mean_x = field(SUM_X, slot) / count
        mean_y = field(SUM_Y, slot) / count
        rel_x = field(WIND_X, slot) - mean_x
        rel_y = field(WIND_Y, slot) - mean_y
        gain = WIND_GAIN * 0.64
        along = [(gain * rel_x) * cosine[k] + (gain * rel_y) * sine[k] for k in range(4)]
        sea = field(SEA, slot)
        damp = jnp.broadcast_to(damping_of(sums, place_row, sea), (lanes, width))
        sea = jnp.broadcast_to(sea, (lanes, width))
        return mean_x, mean_y, along, sea, damp

    own_x, own_y, along_own, sea_own, damp_own = column_state(slot_own, sums_ref, 0)
    mate_x, _, along_mate, sea_mate, damp_mate = column_state(slot_mate, other_sums_ref, 2)
    other_x, _, along_other, sea_other, damp_other = column_state(slot_other, other_sums_ref, 0)
    flow_x = CURRENT_TOP * jnp.tanh(own_x)
    flow_y = CURRENT_TOP * jnp.tanh(own_y)
    sign = jnp.where(odd > 0, 1.0, -1.0)
    face_mate = jnp.broadcast_to(
        (0.5 * sign) * (flow_x + CURRENT_TOP * jnp.tanh(mate_x)), (lanes, width)
    )
    face_other = jnp.broadcast_to(
        (-0.5 * sign) * (flow_x + CURRENT_TOP * jnp.tanh(other_x)), (lanes, width)
    )
    flow_y = jnp.broadcast_to(flow_y, (lanes, width))
    face_north = 0.5 * (flow_y + pltpu.roll(flow_y, width - 1, 1))
    inner = jnp.where(
        lax.broadcasted_iota(jnp.int32, (lanes, width), 1) < width - 1, 1.0, 0.0
    )
    signed_cosine = [sign * cosine[k] for k in range(4)]

    def level_step(index, carry):
        frequency, speed, sums = carry
        sums = list(sums)
        for sub in range(inner_count):
            square = frequency * frequency
            scale_own = sea_own / (1.0 + square * damp_own)
            scale_mate = sea_mate / (1.0 + square * damp_mate)
            scale_other = sea_other / (1.0 + square * damp_other)
            weight = (STOKES_GAIN * 0.1) * (square * square)
            base = (index * inner_count + sub) * NDIR
            for k in range(4):
                rows = pl.ds(pl.multiple_of(base + 8 * k, 8), 8)

                def forced_of(ref, scale, along):
                    grown = jnp.maximum(frequency * along[k] + (1.0 - WIND_GAIN), 1.0)
                    return (ref[rows, :] * scale) * grown

                forced = forced_of(own_ref, scale_own, along_own)
                forced_mate = forced_of(mate_ref, scale_mate, along_mate)
                forced_other = forced_of(other_ref, scale_other, along_other)
                speed_x = speed * signed_cosine[k]
                q_mate = face_mate + speed_x
                q_other = face_other - speed_x
                in_mate = jnp.maximum(q_mate, 0.0)
                in_other = jnp.maximum(q_other, 0.0)
                out = (in_mate - q_mate) + (in_other - q_other)
                north = speed * sine[k] + face_north
                flux = (
                    jnp.maximum(north, 0.0) * forced
                    + jnp.minimum(north, 0.0) * pltpu.roll(forced, width - 1, 1)
                ) * inner
                new = forced - out * forced + (in_mate * forced_mate + in_other * forced_other)
                new = (new - (flux - pltpu.roll(flux, 1, 1))) * sea_own
                updated_ref[rows, :] = new
                sums[k] = sums[k] + weight * new
            frequency = frequency * GROWTH
            speed = speed * (1.0 / GROWTH)
        return frequency, speed, tuple(sums)

    zero = jnp.zeros((lanes, width), jnp.float32)
    start = (jnp.float32(FIRST_FREQ), jnp.float32(SPEED_TOP), (zero,) * 4)
    _, _, sums = lax.fori_loop(0, outer_count, level_step, start)
    drift_x = sums[0] * cosine[0]
    drift_y = sums[0] * sine[0]
    for k in range(1, 4):
        drift_x = drift_x + sums[k] * cosine[k]
        drift_y = drift_y + sums[k] * sine[k]
    drift_ref[0:1, :] = jnp.sum(drift_x, axis=0, keepdims=True)
    drift_ref[1:2, :] = jnp.sum(drift_y, axis=0, keepdims=True)
    drift_ref[2:8, :] = jnp.zeros((6, width), jnp.float32)


def pick_kernel(columns, coupling_ref, own_ref, mate_ref, other_ref, cells_ref):
    width = own_ref.shape[1]
    first, odd, group = place()
    ocean = jnp.where(group > 0, 1.0, 0.0)
    for start in range(0, coupling_ref.shape[1], width):
        part = pl.ds(start, width)
        row, slot = slots_of(coupling_ref[:, part], width, first, columns)
        row = jnp.broadcast_to(row, (8, width))
        own = jnp.take_along_axis(own_ref[...], row, axis=1)[0:2]
        mate = jnp.take_along_axis(mate_ref[...], row, axis=1)[0:2]
        other = jnp.take_along_axis(other_ref[...], row, axis=1)[0:2]
        value = jnp.where(slot == 1 + odd, own, jnp.where(slot == 2 - odd, mate, other))
        cells_ref[:, part] = value * ocean


def direction_table(width):
    heading = np.arange(NDIR) * (2.0 * math.pi / NDIR)
    table = np.concatenate([np.cos(heading), np.sin(heading)]).astype(np.float32)
    return jnp.asarray(np.repeat(table[:, None], width, axis=1))


def body(spectrum, sea_mask, wind, currents, coupling):
    bins, _, width = spectrum.shape
    devices = lax.axis_size("dev")
    groups = lax.axis_size("grp")
    cells = coupling.shape[1]
    mates = [(i, i ^ 1) for i in range(devices)]
    others = [(i, (i + (1 if i % 2 else -1)) % devices) for i in range(devices)]

    def crossed(value, group_step, chip_step):
        def target(group, dev):
            if groups & (groups - 1):
                group = (group + group_step) % groups
            else:
                group = group ^ group_step
            return group * devices + ((dev + 2 * chip_step) % devices ^ 1)

        pairs = [(g * devices + d, target(g, d)) for g in range(groups) for d in range(devices)]
        return lax.ppermute(value, ("grp", "dev"), pairs)

    own = spectrum.reshape(bins, width)
    other = lax.ppermute(own, "dev", others)
    mate = lax.ppermute(own, "dev", mates)

    anywhere = pl.BlockSpec(memory_space=pl.ANY)
    band = pl.pallas_call(
        functools.partial(band_kernel, devices),
        out_shape=pltpu.VMEM((FIELDS * SLOTS, width), jnp.float32),
        in_specs=[anywhere] * 4,
        out_specs=VMEM,
        scratch_shapes=[
            pltpu.VMEM((1, cells), jnp.int32),
            pltpu.VMEM((2, cells), jnp.float32),
            pltpu.VMEM((1, width), jnp.int32),
            pltpu.VMEM((2, width), jnp.float32),
            pltpu.SemaphoreType.DMA((4,)),
        ],
    )(coupling, currents[0], sea_mask, wind[:, 0])
    band = band + lax.ppermute(band, "dev", mates)
    parts = [crossed(band, step, 0) for step in range(1, groups)]
    for part in parts:
        band = band + part
    after = crossed(band, 0, -1)
    before = crossed(band, 0, 1)

    own_near, sums = pl.pallas_call(
        fetch_kernel,
        out_shape=(
            pltpu.VMEM((bins, width), jnp.float32),
            pltpu.VMEM((8, width), jnp.float32),
        ),
        in_specs=[anywhere, VMEM],
        out_specs=(VMEM, VMEM),
        scratch_shapes=[pltpu.SemaphoreType.DMA],
    )(own, *near(band))
    updated, drift = pl.pallas_call(
        step_kernel,
        out_shape=(
            pltpu.VMEM((bins, width), jnp.float32),
            pltpu.VMEM((8, width), jnp.float32),
        ),
        in_specs=[VMEM] * 8,
        out_specs=(VMEM, VMEM),
        scratch_shapes=[pltpu.VMEM((8, width), jnp.float32)],
    )(*near(direction_table(width), own_near, sums, mate, other, band, after, before))

    drift_other = lax.ppermute(drift, "dev", others)
    drift_mate = lax.ppermute(drift, "dev", mates)
    cell_drift = pl.pallas_call(
        functools.partial(pick_kernel, devices),
        out_shape=jax.ShapeDtypeStruct(currents.shape[1:], jnp.float32),
        in_specs=[VMEM] * 4,
        out_specs=VMEM,
    )(*near(coupling, drift, drift_mate, drift_other))
    return updated.reshape(spectrum.shape), cell_drift[None]


def solution(mesh):
    return jax.shard_map(
        body,
        mesh=mesh,
        in_specs=(
            P(None, "dev", None),
            P("dev", None),
            P(None, "dev", None),
            P("grp", None, "dev"),
            P("grp", "dev"),
        ),
        out_specs=(P(None, "dev", None), P("grp", None, "dev")),
        check_vma=False,
    )
```

```python
import functools
import math

import jax
import jax.numpy as jnp
import numpy as np
from jax import lax
from jax.experimental import pallas as pl
from jax.experimental.pallas import tpu as pltpu
from jax.sharding import PartitionSpec as P

NDIR = 32
FIRST_FREQ = 0.04
GROWTH = 1.1
SPEED_TOP = 0.45
CURRENT_TOP = 0.2
WIND_GAIN = 0.03
WHITECAP = 0.3
STEEP_SCALE = 0.4
STOKES_GAIN = 3.0

SLOTS = 4
FIELDS = 6
SUM_X, SUM_Y, COUNT, SEA, WIND_X, WIND_Y = range(FIELDS)
VMEM = pl.BlockSpec(memory_space=pltpu.VMEM)


def near(*arrays):
    return [pltpu.with_memory_space_constraint(array, pltpu.VMEM) for array in arrays]


def place():
    me = lax.axis_index("dev")
    odd = lax.rem(me, 2)
    return me - odd - 1, odd, lax.axis_index("grp")


def padded(levels):
    return -(-levels // 8) * 8


def level_groups(levels):
    for size in (36, 18, 12, 6, 4, 3, 2):
        if levels % size == 0:
            return levels // size, size
    return levels, 1


def slots_of(coupling, width, first, columns):
    col = lax.div(coupling, jnp.int32(width))
    row = coupling - col * width
    slot = col - first
    slot = jnp.where(slot < 0, slot + columns, slot)
    slot = jnp.where(slot >= columns, slot - columns, slot)
    return row, slot


def band_kernel(
    columns, coupling_hbm, currents_hbm, sea_hbm, wind_hbm, band_ref,
    coupling_ref, currents_ref, sea_ref, wind_ref, sems,
):
    width = band_ref.shape[1]
    first, odd, group = place()
    is_ocean = group > 0

    @pl.when(is_ocean)
    def _():
        copies = [
            pltpu.make_async_copy(coupling_hbm, coupling_ref, sems.at[0]),
            pltpu.make_async_copy(currents_hbm, currents_ref, sems.at[1]),
        ]
        for copy in copies:
            copy.start()
        for copy in copies:
            copy.wait()
        row, slot = slots_of(coupling_ref[...], width, first, columns)
        cells = row.shape[1]
        parts_x, parts_y = [], []
        for comp, parts in ((0, parts_x), (1, parts_y)):
            rest = currents_ref[comp : comp + 1, :]
            for _ in range(3):
                part = rest.astype(jnp.bfloat16).astype(jnp.float32)
                parts.append(part)
                rest = rest - part
        slot_id = lax.broadcasted_iota(jnp.int32, (SLOTS, cells), 0)
        here = jnp.where(slot_id == slot, 1.0, 0.0)
        rows = []
        for part in range(3):
            rows += [here * parts_x[part], here * parts_y[part]]
        rows += [here, jnp.zeros_like(here)]
        values = jnp.concatenate(rows, axis=0).astype(jnp.bfloat16)
        row_id = lax.broadcasted_iota(jnp.int32, (width, cells), 0)
        hot = jnp.where(row_id == row, 1.0, 0.0).astype(jnp.bfloat16)
        sums = lax.dot_general(
            values, hot, (((1,), (1,)), ((), ())), preferred_element_type=jnp.float32
        )
        step = 2 * SLOTS
        band_ref[0:step, :] = sums[0:step] + sums[step : 2 * step] + sums[2 * step : 3 * step]
        band_ref[step : 2 * step, :] = sums[3 * step : 4 * step]
        band_ref[2 * step : 3 * step, :] = jnp.zeros((step, width), jnp.float32)

    @pl.when(jnp.logical_not(is_ocean))
    def _():
        copies = [
            pltpu.make_async_copy(sea_hbm, sea_ref, sems.at[2]),
            pltpu.make_async_copy(wind_hbm, wind_ref, sems.at[3]),
        ]
        for copy in copies:
            copy.start()
        band_ref[...] = jnp.zeros_like(band_ref)
        for copy in copies:
            copy.wait()
        own = odd + 1
        band_ref[pl.ds(SEA * SLOTS + own, 1), :] = sea_ref[...].astype(jnp.float32)
        band_ref[pl.ds(WIND_X * SLOTS + own, 1), :] = wind_ref[0:1, :]
        band_ref[pl.ds(WIND_Y * SLOTS + own, 1), :] = wind_ref[1:2, :]


def spectrum_sums(ref, sums_ref, first_row):
    bins, width = ref.shape
    total = jnp.zeros((8, width), jnp.float32)
    moment = jnp.zeros((8, width), jnp.float32)
    for level in range(bins // NDIR):
        frequency = FIRST_FREQ * GROWTH**level
        block = ref[level * NDIR : (level + 1) * NDIR, :]
        block = block[0:8] + block[8:16] + (block[16:24] + block[24:32])
        total += (0.1 * frequency) * block
        moment += (0.1 * frequency * frequency) * block
    sums_ref[first_row : first_row + 1, :] = jnp.sum(total, axis=0, keepdims=True)
    sums_ref[first_row + 1 : first_row + 2, :] = jnp.sum(moment, axis=0, keepdims=True)


def fetch_kernel(own_hbm, _, own_ref, sums_ref, sem):
    fetch = pltpu.make_async_copy(own_hbm, own_ref, sem)
    fetch.start()
    sums_ref[...] = jnp.zeros_like(sums_ref)
    fetch.wait()
    spectrum_sums(own_ref, sums_ref, 0)


def damping_of(sums_ref, place_row, sea):
    total = sums_ref[place_row : place_row + 1, :] * sea
    moment = sums_ref[place_row + 1 : place_row + 2, :] * sea
    is_sea = sea > 0.5
    mean_freq = jnp.where(is_sea, moment / jnp.where(is_sea, total, 1.0), 1.0)
    square = mean_freq * mean_freq
    steep = STEEP_SCALE * total * (square * square)
    return WHITECAP * (steep * steep) / square


def step_kernel(
    table_ref, own_ref, sums_ref, mate_ref, other_ref, band_ref, after_ref, before_ref, updated_ref, drift_ref,
    other_sums_ref, scale_ref,
):
    bins, width = own_ref.shape
    lanes = 8
    spectrum_sums(mate_ref, other_sums_ref, 2)
    spectrum_sums(other_ref, other_sums_ref, 0)
    outer_count, inner_count = level_groups(bins // NDIR)
    _, odd, _ = place()
    slot_own, slot_mate, slot_other = 1 + odd, 2 - odd, 3 * odd

    def field(index, slot):
        base = index * SLOTS
        value = band_ref[pl.ds(base + slot, 1), :]
        low = before_ref[pl.ds(base + jnp.minimum(slot, 1) + 2, 1), :]
        high = after_ref[pl.ds(base + jnp.maximum(slot, 2) - 2, 1), :]
        return value + jnp.where(slot < 2, low, high)

    cosine = [table_ref[8 * k : 8 * k + 8, :] for k in range(4)]
    sine = [table_ref[NDIR + 8 * k : NDIR + 8 * k + 8, :] for k in range(4)]

    steps = padded(bins // NDIR)

    def column_state(slot, sums, place_row):
        count = jnp.maximum(field(COUNT, slot), 1.0)
        mean_x = field(SUM_X, slot) / count
        mean_y = field(SUM_Y, slot) / count
        rel_x = field(WIND_X, slot) - mean_x
        rel_y = field(WIND_Y, slot) - mean_y
        gain = WIND_GAIN * 0.64
        along = [(gain * rel_x) * cosine[k] + (gain * rel_y) * sine[k] for k in range(4)]
        sea = field(SEA, slot)
        squares = table_ref[2 * NDIR : 2 * NDIR + steps, :]
        scale = sea / (1.0 + squares * damping_of(sums, place_row, sea))
        return mean_x, mean_y, along, sea, scale

    own_x, own_y, along_own, sea_own, scale = column_state(slot_own, sums_ref, 0)
    scale_ref[0 * steps : 1 * steps, :] = scale
    mate_x, _, along_mate, sea_mate, scale = column_state(slot_mate, other_sums_ref, 2)
    scale_ref[1 * steps : 2 * steps, :] = scale
    other_x, _, along_other, sea_other, scale = column_state(slot_other, other_sums_ref, 0)
    scale_ref[2 * steps : 3 * steps, :] = scale
    flow_x = CURRENT_TOP * jnp.tanh(own_x)
    flow_y = CURRENT_TOP * jnp.tanh(own_y)
    sign = jnp.where(odd > 0, 1.0, -1.0)
    face_mate = jnp.broadcast_to(
        (0.5 * sign) * (flow_x + CURRENT_TOP * jnp.tanh(mate_x)), (lanes, width)
    )
    face_other = jnp.broadcast_to(
        (-0.5 * sign) * (flow_x + CURRENT_TOP * jnp.tanh(other_x)), (lanes, width)
    )
    flow_y = jnp.broadcast_to(flow_y, (lanes, width))
    inner = jnp.where(
        lax.broadcasted_iota(jnp.int32, (lanes, width), 1) < width - 1, 1.0, 0.0
    )
    face_north = (0.5 * inner) * (flow_y + pltpu.roll(flow_y, width - 1, 1))
    inner_sine = [inner * sine[k] for k in range(4)]
    sea_own = jnp.broadcast_to(sea_own, (lanes, width))
    face_sum = face_mate + face_other
    signed_cosine = [sign * cosine[k] for k in range(4)]

    def level_step(index, carry):
        frequency, speed, sums = carry
        sums = list(sums)
        for sub in range(inner_count):
            square = frequency * frequency
            level = index * inner_count + sub
            scale_own, scale_mate, scale_other = (
                jnp.broadcast_to(scale_ref[pl.ds(column * steps + level, 1), :], (lanes, width))
                for column in range(3)
            )
            weight = (STOKES_GAIN * 0.1) * (square * square)
            base = level * NDIR
            for k in range(4):
                rows = pl.ds(pl.multiple_of(base + 8 * k, 8), 8)

                def forced_of(ref, scale, along):
                    grown = jnp.maximum(frequency * along[k] + (1.0 - WIND_GAIN), 1.0)
                    return (ref[rows, :] * scale) * grown

                forced = forced_of(own_ref, scale_own, along_own)
                forced_mate = forced_of(mate_ref, scale_mate, along_mate)
                forced_other = forced_of(other_ref, scale_other, along_other)
                speed_x = speed * signed_cosine[k]
                q_mate = face_mate + speed_x
                q_other = face_other - speed_x
                in_mate = jnp.maximum(q_mate, 0.0)
                in_other = jnp.maximum(q_other, 0.0)
                out = (in_mate + in_other) - face_sum
                north = speed * inner_sine[k] + face_north
                flux = jnp.maximum(north, 0.0) * forced
                flux = flux + jnp.minimum(north, 0.0) * pltpu.roll(forced, width - 1, 1)
                new = forced - out * forced + (in_mate * forced_mate + in_other * forced_other)
                new = (new - (flux - pltpu.roll(flux, 1, 1))) * sea_own
                updated_ref[rows, :] = new
                sums[k] = sums[k] + weight * new
            frequency = frequency * GROWTH
            speed = speed * (1.0 / GROWTH)
        return frequency, speed, tuple(sums)

    zero = jnp.zeros((lanes, width), jnp.float32)
    start = (jnp.float32(FIRST_FREQ), jnp.float32(SPEED_TOP), (zero,) * 4)
    _, _, sums = lax.fori_loop(0, outer_count, level_step, start)
    drift_x = sums[0] * cosine[0]
    drift_y = sums[0] * sine[0]
    for k in range(1, 4):
        drift_x = drift_x + sums[k] * cosine[k]
        drift_y = drift_y + sums[k] * sine[k]
    drift_ref[0:1, :] = jnp.sum(drift_x, axis=0, keepdims=True)
    drift_ref[1:2, :] = jnp.sum(drift_y, axis=0, keepdims=True)
    drift_ref[2:8, :] = jnp.zeros((6, width), jnp.float32)


def pick_kernel(columns, coupling_ref, own_ref, mate_ref, other_ref, cells_ref):
    width = own_ref.shape[1]
    first, odd, group = place()
    ocean = jnp.where(group > 0, 1.0, 0.0)
    for start in range(0, coupling_ref.shape[1], width):
        part = pl.ds(start, width)
        row, slot = slots_of(coupling_ref[:, part], width, first, columns)
        row = jnp.broadcast_to(row, (8, width))
        own = jnp.take_along_axis(own_ref[...], row, axis=1)[0:2]
        mate = jnp.take_along_axis(mate_ref[...], row, axis=1)[0:2]
        other = jnp.take_along_axis(other_ref[...], row, axis=1)[0:2]
        value = jnp.where(slot == 1 + odd, own, jnp.where(slot == 2 - odd, mate, other))
        cells_ref[:, part] = value * ocean


def direction_table(bins, width):
    heading = np.arange(NDIR) * (2.0 * math.pi / NDIR)
    table = np.concatenate([np.cos(heading), np.sin(heading)]).astype(np.float32)
    levels = np.minimum(np.arange(padded(bins // NDIR)), bins // NDIR - 1)
    squares = ((FIRST_FREQ * GROWTH**levels) ** 2).astype(np.float32)
    table = np.concatenate([table, squares])
    return jnp.asarray(np.repeat(table[:, None], width, axis=1))


def body(spectrum, sea_mask, wind, currents, coupling):
    bins, _, width = spectrum.shape
    devices = lax.axis_size("dev")
    groups = lax.axis_size("grp")
    cells = coupling.shape[1]
    mates = [(i, i ^ 1) for i in range(devices)]
    others = [(i, (i + (1 if i % 2 else -1)) % devices) for i in range(devices)]

    def crossed(value, group_step, chip_step):
        def target(group, dev):
            if groups & (groups - 1):
                group = (group + group_step) % groups
            else:
                group = group ^ group_step
            return group * devices + ((dev + 2 * chip_step) % devices ^ 1)

        pairs = [(g * devices + d, target(g, d)) for g in range(groups) for d in range(devices)]
        return lax.ppermute(value, ("grp", "dev"), pairs)

    own = spectrum.reshape(bins, width)
    other = lax.ppermute(own, "dev", others)
    mate = lax.ppermute(own, "dev", mates)

    anywhere = pl.BlockSpec(memory_space=pl.ANY)
    band = pl.pallas_call(
        functools.partial(band_kernel, devices),
        out_shape=pltpu.VMEM((FIELDS * SLOTS, width), jnp.float32),
        in_specs=[anywhere] * 4,
        out_specs=VMEM,
        scratch_shapes=[
            pltpu.VMEM((1, cells), jnp.int32),
            pltpu.VMEM((2, cells), jnp.float32),
            pltpu.VMEM((1, width), jnp.int32),
            pltpu.VMEM((2, width), jnp.float32),
            pltpu.SemaphoreType.DMA((4,)),
        ],
    )(coupling, currents[0], sea_mask, wind[:, 0])
    band = band + lax.ppermute(band, "dev", mates)
    parts = [crossed(band, step, 0) for step in range(1, groups)]
    for part in parts:
        band = band + part
    after = crossed(band, 0, -1)
    before = crossed(band, 0, 1)

    own_near, sums = pl.pallas_call(
        fetch_kernel,
        out_shape=(
            pltpu.VMEM((bins, width), jnp.float32),
            pltpu.VMEM((8, width), jnp.float32),
        ),
        in_specs=[anywhere, VMEM],
        out_specs=(VMEM, VMEM),
        scratch_shapes=[pltpu.SemaphoreType.DMA],
    )(own, *near(band))
    updated, drift = pl.pallas_call(
        step_kernel,
        out_shape=(
            pltpu.VMEM((bins, width), jnp.float32),
            pltpu.VMEM((8, width), jnp.float32),
        ),
        in_specs=[VMEM] * 8,
        out_specs=(VMEM, VMEM),
        scratch_shapes=[
            pltpu.VMEM((8, width), jnp.float32),
            pltpu.VMEM((3 * padded(bins // NDIR), width), jnp.float32),
        ],
    )(*near(direction_table(bins, width), own_near, sums, mate, other, band, after, before))

    drift_other = lax.ppermute(drift, "dev", others)
    drift_mate = lax.ppermute(drift, "dev", mates)
    cell_drift = pl.pallas_call(
        functools.partial(pick_kernel, devices),
        out_shape=jax.ShapeDtypeStruct(currents.shape[1:], jnp.float32),
        in_specs=[VMEM] * 4,
        out_specs=VMEM,
    )(*near(coupling, drift, drift_mate, drift_other))
    return updated.reshape(spectrum.shape), cell_drift[None]


def solution(mesh):
    return jax.shard_map(
        body,
        mesh=mesh,
        in_specs=(
            P(None, "dev", None),
            P("dev", None),
            P(None, "dev", None),
            P("grp", None, "dev"),
            P("grp", "dev"),
        ),
        out_specs=(P(None, "dev", None), P("grp", None, "dev")),
        check_vma=False,
    )
```

```python
import functools
import math

import jax
import jax.numpy as jnp
import numpy as np
from jax import lax
from jax.experimental import pallas as pl
from jax.experimental.pallas import tpu as pltpu
from jax.sharding import PartitionSpec as P

NDIR = 32
FIRST_FREQ = 0.04
GROWTH = 1.1
SPEED_TOP = 0.45
CURRENT_TOP = 0.2
WIND_GAIN = 0.03
WHITECAP = 0.3
STEEP_SCALE = 0.4
STOKES_GAIN = 3.0

SLOTS = 4
FIELDS = 6
SUM_X, SUM_Y, COUNT, SEA, WIND_X, WIND_Y = range(FIELDS)
VMEM = pl.BlockSpec(memory_space=pltpu.VMEM)


def near(*arrays):
    return [pltpu.with_memory_space_constraint(array, pltpu.VMEM) for array in arrays]


def place():
    me = lax.axis_index("dev")
    odd = lax.rem(me, 2)
    return me - odd - 1, odd, lax.axis_index("grp")


def padded(levels):
    return -(-levels // 8) * 8


def level_groups(levels):
    for size in (36, 18, 12, 6, 4, 3, 2):
        if levels % size == 0:
            return levels // size, size
    return levels, 1


def slots_of(coupling, width, first, columns):
    col = lax.div(coupling, jnp.int32(width))
    row = coupling - col * width
    slot = col - first
    slot = jnp.where(slot < 0, slot + columns, slot)
    slot = jnp.where(slot >= columns, slot - columns, slot)
    return row, slot


def band_kernel(
    columns, coupling_hbm, currents_hbm, sea_hbm, wind_hbm, band_ref,
    coupling_ref, currents_ref, sea_ref, wind_ref, sems,
):
    width = band_ref.shape[1]
    first, odd, group = place()
    is_ocean = group > 0

    @pl.when(is_ocean)
    def _():
        copies = [
            pltpu.make_async_copy(coupling_hbm, coupling_ref, sems.at[0]),
            pltpu.make_async_copy(currents_hbm, currents_ref, sems.at[1]),
        ]
        for copy in copies:
            copy.start()
        for copy in copies:
            copy.wait()
        row, slot = slots_of(coupling_ref[...], width, first, columns)
        cells = row.shape[1]
        parts_x, parts_y = [], []
        for comp, parts in ((0, parts_x), (1, parts_y)):
            rest = currents_ref[comp : comp + 1, :]
            for _ in range(3):
                part = rest.astype(jnp.bfloat16).astype(jnp.float32)
                parts.append(part)
                rest = rest - part
        slot_id = lax.broadcasted_iota(jnp.int32, (SLOTS, cells), 0)
        here = jnp.where(slot_id == slot, 1.0, 0.0)
        rows = []
        for part in range(3):
            rows += [here * parts_x[part], here * parts_y[part]]
        rows += [here, jnp.zeros_like(here)]
        values = jnp.concatenate(rows, axis=0).astype(jnp.bfloat16)
        row_id = lax.broadcasted_iota(jnp.int32, (width, cells), 0)
        hot = jnp.where(row_id == row, 1.0, 0.0).astype(jnp.bfloat16)
        sums = lax.dot_general(
            values, hot, (((1,), (1,)), ((), ())), preferred_element_type=jnp.float32
        )
        step = 2 * SLOTS
        band_ref[0:step, :] = sums[0:step] + sums[step : 2 * step] + sums[2 * step : 3 * step]
        band_ref[step : 2 * step, :] = sums[3 * step : 4 * step]
        band_ref[2 * step : 3 * step, :] = jnp.zeros((step, width), jnp.float32)

    @pl.when(jnp.logical_not(is_ocean))
    def _():
        copies = [
            pltpu.make_async_copy(sea_hbm, sea_ref, sems.at[2]),
            pltpu.make_async_copy(wind_hbm, wind_ref, sems.at[3]),
        ]
        for copy in copies:
            copy.start()
        band_ref[...] = jnp.zeros_like(band_ref)
        for copy in copies:
            copy.wait()
        own = odd + 1
        band_ref[pl.ds(SEA * SLOTS + own, 1), :] = sea_ref[...].astype(jnp.float32)
        band_ref[pl.ds(WIND_X * SLOTS + own, 1), :] = wind_ref[0:1, :]
        band_ref[pl.ds(WIND_Y * SLOTS + own, 1), :] = wind_ref[1:2, :]


def spectrum_sums(ref, sums_ref, first_row):
    bins, width = ref.shape
    total = jnp.zeros((8, width), jnp.float32)
    moment = jnp.zeros((8, width), jnp.float32)
    for level in range(bins // NDIR):
        frequency = FIRST_FREQ * GROWTH**level
        block = ref[level * NDIR : (level + 1) * NDIR, :]
        block = block[0:8] + block[8:16] + (block[16:24] + block[24:32])
        total += (0.1 * frequency) * block
        moment += (0.1 * frequency * frequency) * block
    sums_ref[first_row : first_row + 1, :] = jnp.sum(total, axis=0, keepdims=True)
    sums_ref[first_row + 1 : first_row + 2, :] = jnp.sum(moment, axis=0, keepdims=True)


def fetch_kernel(own_hbm, _, own_ref, sums_ref, sem):
    fetch = pltpu.make_async_copy(own_hbm, own_ref, sem)
    fetch.start()
    sums_ref[...] = jnp.zeros_like(sums_ref)
    fetch.wait()
    spectrum_sums(own_ref, sums_ref, 0)


def halo_kernel(mate_ref, other_ref, sums_ref):
    sums_ref[...] = jnp.zeros_like(sums_ref)
    spectrum_sums(other_ref, sums_ref, 0)
    spectrum_sums(mate_ref, sums_ref, 2)


def damping_of(sums_ref, place_row, sea):
    total = sums_ref[place_row : place_row + 1, :] * sea
    moment = sums_ref[place_row + 1 : place_row + 2, :] * sea
    is_sea = sea > 0.5
    mean_freq = jnp.where(is_sea, moment / jnp.where(is_sea, total, 1.0), 1.0)
    square = mean_freq * mean_freq
    steep = STEEP_SCALE * total * (square * square)
    return WHITECAP * (steep * steep) / square


def step_kernel(
    table_ref, own_ref, sums_ref, other_sums_ref, mate_ref, other_ref, band_ref, after_ref, before_ref, updated_ref, drift_ref,
    scale_ref,
):
    bins, width = own_ref.shape
    lanes = 8
    outer_count, inner_count = level_groups(bins // NDIR)
    _, odd, _ = place()
    slot_own, slot_mate, slot_other = 1 + odd, 2 - odd, 3 * odd

    def field(index, slot):
        base = index * SLOTS
        value = band_ref[pl.ds(base + slot, 1), :]
        low = before_ref[pl.ds(base + jnp.minimum(slot, 1) + 2, 1), :]
        high = after_ref[pl.ds(base + jnp.maximum(slot, 2) - 2, 1), :]
        return value + jnp.where(slot < 2, low, high)

    cosine = [table_ref[8 * k : 8 * k + 8, :] for k in range(4)]
    sine = [table_ref[NDIR + 8 * k : NDIR + 8 * k + 8, :] for k in range(4)]

    steps = padded(bins // NDIR)

    def column_state(slot, sums, place_row):
        count = jnp.maximum(field(COUNT, slot), 1.0)
        mean_x = field(SUM_X, slot) / count
        mean_y = field(SUM_Y, slot) / count
        rel_x = field(WIND_X, slot) - mean_x
        rel_y = field(WIND_Y, slot) - mean_y
        gain = WIND_GAIN * 0.64
        along = [(gain * rel_x) * cosine[k] + (gain * rel_y) * sine[k] for k in range(4)]
        sea = field(SEA, slot)
        squares = table_ref[2 * NDIR : 2 * NDIR + steps, :]
        scale = sea / (1.0 + squares * damping_of(sums, place_row, sea))
        return mean_x, mean_y, along, sea, scale

    own_x, own_y, along_own, sea_own, scale = column_state(slot_own, sums_ref, 0)
    scale_ref[0 * steps : 1 * steps, :] = scale
    mate_x, _, along_mate, sea_mate, scale = column_state(slot_mate, other_sums_ref, 2)
    scale_ref[1 * steps : 2 * steps, :] = scale
    other_x, _, along_other, sea_other, scale = column_state(slot_other, other_sums_ref, 0)
    scale_ref[2 * steps : 3 * steps, :] = scale
    flow_x = CURRENT_TOP * jnp.tanh(own_x)
    flow_y = CURRENT_TOP * jnp.tanh(own_y)
    sign = jnp.where(odd > 0, 1.0, -1.0)
    face_mate = jnp.broadcast_to(
        (0.5 * sign) * (flow_x + CURRENT_TOP * jnp.tanh(mate_x)), (lanes, width)
    )
    face_other = jnp.broadcast_to(
        (-0.5 * sign) * (flow_x + CURRENT_TOP * jnp.tanh(other_x)), (lanes, width)
    )
    flow_y = jnp.broadcast_to(flow_y, (lanes, width))
    inner = jnp.where(
        lax.broadcasted_iota(jnp.int32, (lanes, width), 1) < width - 1, 1.0, 0.0
    )
    face_north = (0.5 * inner) * (flow_y + pltpu.roll(flow_y, width - 1, 1))
    inner_sine = [inner * sine[k] for k in range(4)]
    sea_own = jnp.broadcast_to(sea_own, (lanes, width))
    face_sum = face_mate + face_other
    signed_cosine = [sign * cosine[k] for k in range(4)]

    def level_step(index, carry):
        frequency, speed, sums = carry
        sums = list(sums)
        for sub in range(inner_count):
            square = frequency * frequency
            level = index * inner_count + sub
            scale_own, scale_mate, scale_other = (
                jnp.broadcast_to(scale_ref[pl.ds(column * steps + level, 1), :], (lanes, width))
                for column in range(3)
            )
            weight = (STOKES_GAIN * 0.1) * (square * square)
            base = level * NDIR
            for k in range(4):
                rows = pl.ds(pl.multiple_of(base + 8 * k, 8), 8)

                def forced_of(ref, scale, along):
                    grown = jnp.maximum(frequency * along[k] + (1.0 - WIND_GAIN), 1.0)
                    return (ref[rows, :] * scale) * grown

                forced = forced_of(own_ref, scale_own, along_own)
                forced_mate = forced_of(mate_ref, scale_mate, along_mate)
                forced_other = forced_of(other_ref, scale_other, along_other)
                speed_x = speed * signed_cosine[k]
                q_mate = face_mate + speed_x
                q_other = face_other - speed_x
                in_mate = jnp.maximum(q_mate, 0.0)
                in_other = jnp.maximum(q_other, 0.0)
                out = (in_mate + in_other) - face_sum
                north = speed * inner_sine[k] + face_north
                flux = jnp.maximum(north, 0.0) * forced
                flux = flux + jnp.minimum(north, 0.0) * pltpu.roll(forced, width - 1, 1)
                new = forced - out * forced + (in_mate * forced_mate + in_other * forced_other)
                new = (new - (flux - pltpu.roll(flux, 1, 1))) * sea_own
                updated_ref[rows, :] = new
                sums[k] = sums[k] + weight * new
            frequency = frequency * GROWTH
            speed = speed * (1.0 / GROWTH)
        return frequency, speed, tuple(sums)

    zero = jnp.zeros((lanes, width), jnp.float32)
    start = (jnp.float32(FIRST_FREQ), jnp.float32(SPEED_TOP), (zero,) * 4)
    _, _, sums = lax.fori_loop(0, outer_count, level_step, start)
    drift_x = sums[0] * cosine[0]
    drift_y = sums[0] * sine[0]
    for k in range(1, 4):
        drift_x = drift_x + sums[k] * cosine[k]
        drift_y = drift_y + sums[k] * sine[k]
    drift_ref[0:1, :] = jnp.sum(drift_x, axis=0, keepdims=True)
    drift_ref[1:2, :] = jnp.sum(drift_y, axis=0, keepdims=True)
    drift_ref[2:8, :] = jnp.zeros((6, width), jnp.float32)


def pick_kernel(columns, coupling_ref, own_ref, mate_ref, other_ref, cells_ref):
    width = own_ref.shape[1]
    first, odd, group = place()
    ocean = jnp.where(group > 0, 1.0, 0.0)
    for start in range(0, coupling_ref.shape[1], width):
        part = pl.ds(start, width)
        row, slot = slots_of(coupling_ref[:, part], width, first, columns)
        row = jnp.broadcast_to(row, (8, width))
        own = jnp.take_along_axis(own_ref[...], row, axis=1)[0:2]
        mate = jnp.take_along_axis(mate_ref[...], row, axis=1)[0:2]
        other = jnp.take_along_axis(other_ref[...], row, axis=1)[0:2]
        value = jnp.where(slot == 1 + odd, own, jnp.where(slot == 2 - odd, mate, other))
        cells_ref[:, part] = value * ocean


def direction_table(bins, width):
    heading = np.arange(NDIR) * (2.0 * math.pi / NDIR)
    table = np.concatenate([np.cos(heading), np.sin(heading)]).astype(np.float32)
    levels = np.minimum(np.arange(padded(bins // NDIR)), bins // NDIR - 1)
    squares = ((FIRST_FREQ * GROWTH**levels) ** 2).astype(np.float32)
    table = np.concatenate([table, squares])
    return jnp.asarray(np.repeat(table[:, None], width, axis=1))


def body(spectrum, sea_mask, wind, currents, coupling):
    bins, _, width = spectrum.shape
    devices = lax.axis_size("dev")
    groups = lax.axis_size("grp")
    cells = coupling.shape[1]
    mates = [(i, i ^ 1) for i in range(devices)]
    others = [(i, (i + (1 if i % 2 else -1)) % devices) for i in range(devices)]

    def crossed(value, group_step, chip_step):
        def target(group, dev):
            if groups & (groups - 1):
                group = (group + group_step) % groups
            else:
                group = group ^ group_step
            return group * devices + ((dev + 2 * chip_step) % devices ^ 1)

        pairs = [(g * devices + d, target(g, d)) for g in range(groups) for d in range(devices)]
        return lax.ppermute(value, ("grp", "dev"), pairs)

    own = spectrum.reshape(bins, width)
    other = lax.ppermute(own, "dev", others)
    mate = lax.ppermute(own, "dev", mates)

    anywhere = pl.BlockSpec(memory_space=pl.ANY)
    band = pl.pallas_call(
        functools.partial(band_kernel, devices),
        out_shape=pltpu.VMEM((FIELDS * SLOTS, width), jnp.float32),
        in_specs=[anywhere] * 4,
        out_specs=VMEM,
        scratch_shapes=[
            pltpu.VMEM((1, cells), jnp.int32),
            pltpu.VMEM((2, cells), jnp.float32),
            pltpu.VMEM((1, width), jnp.int32),
            pltpu.VMEM((2, width), jnp.float32),
            pltpu.SemaphoreType.DMA((4,)),
        ],
    )(coupling, currents[0], sea_mask, wind[:, 0])
    band = band + lax.ppermute(band, "dev", mates)
    parts = [crossed(band, step, 0) for step in range(1, groups)]
    for part in parts:
        band = band + part
    after = crossed(band, 0, -1)
    before = crossed(band, 0, 1)

    own_near, sums = pl.pallas_call(
        fetch_kernel,
        out_shape=(
            pltpu.VMEM((bins, width), jnp.float32),
            pltpu.VMEM((8, width), jnp.float32),
        ),
        in_specs=[anywhere, VMEM],
        out_specs=(VMEM, VMEM),
        scratch_shapes=[pltpu.SemaphoreType.DMA],
    )(own, *near(band))
    halo_sums = pl.pallas_call(
        halo_kernel,
        out_shape=pltpu.VMEM((8, width), jnp.float32),
        in_specs=[VMEM] * 2,
        out_specs=VMEM,
    )(*near(mate, other))
    updated, drift = pl.pallas_call(
        step_kernel,
        out_shape=(
            pltpu.VMEM((bins, width), jnp.float32),
            pltpu.VMEM((8, width), jnp.float32),
        ),
        in_specs=[VMEM] * 9,
        out_specs=(VMEM, VMEM),
        scratch_shapes=[
            pltpu.VMEM((3 * padded(bins // NDIR), width), jnp.float32),
        ],
    )(*near(direction_table(bins, width), own_near, sums, halo_sums, mate, other, band, after, before))

    drift_other = lax.ppermute(drift, "dev", others)
    drift_mate = lax.ppermute(drift, "dev", mates)
    cell_drift = pl.pallas_call(
        functools.partial(pick_kernel, devices),
        out_shape=jax.ShapeDtypeStruct(currents.shape[1:], jnp.float32),
        in_specs=[VMEM] * 4,
        out_specs=VMEM,
    )(*near(coupling, drift, drift_mate, drift_other))
    return updated.reshape(spectrum.shape), cell_drift[None]


def solution(mesh):
    return jax.shard_map(
        body,
        mesh=mesh,
        in_specs=(
            P(None, "dev", None),
            P("dev", None),
            P(None, "dev", None),
            P("grp", None, "dev"),
            P("grp", "dev"),
        ),
        out_specs=(P(None, "dev", None), P("grp", None, "dev")),
        check_vma=False,
    )
```
